256 devices in a mesh: ta: 8 (over y, core), ha: 2 (over z_lo), wa: 4 (over z_hi), head: 4 (over x).
Axes of the slice: x: 4, y: 4, z: 8 (z_hi: 4, z_lo: 2; z = z_hi * 2 + z_lo), core: 2. Of those that a mesh axis runs over, the one named last changes fastest.
Arguments:
- query: bfloat16 [24, 16, 32, 1536], P('ta', 'ha', 'wa', 'head'), may hold values from -30 to 30
- keys: bfloat16 [24, 16, 32, 1536], P('ta', 'ha', 'wa', 'head'), may hold values from -30 to 30
- values: bfloat16 [24, 16, 32, 1536], P('ta', 'ha', 'wa', 'head'), may hold values from -6 to 6
- grad_out: bfloat16 [24, 16, 32, 1536], P('ta', 'ha', 'wa', 'head'), may hold values from -6 to 6
- text_keys: bfloat16 [256, 1536], P(None, 'head'), may hold values from -6 to 6
- text_values: bfloat16 [256, 1536], P(None, 'head'), may hold values from -6 to 6
- window: int32 [12, 3], P('head'), may hold values from 0 to 1, as said below
Outputs:
- out: bfloat16 [24, 16, 32, 1536], P('ta', 'ha', 'wa', 'head')
- query_grad: bfloat16 [24, 16, 32, 1536], P('ta', 'ha', 'wa', 'head')
- key_grad: bfloat16 [24, 16, 32, 1536], P('ta', 'ha', 'wa', 'head')
- value_grad: bfloat16 [24, 16, 32, 1536], P('ta', 'ha', 'wa', 'head')
- text_key_grad: bfloat16 [256, 1536], P(('ta', 'ha', 'wa'), 'head')
- text_value_grad: bfloat16 [256, 1536], P(('ta', 'ha', 'wa'), 'head')
The draws below stay inside these ranges and needn't reach their ends.
Inputs may be any that keep to these rules, and one draw needn't show every extreme that they name: Each entry is the reach of a head's window in tiles; some head reaches 1 along every axis.
All inputs are finite; a program needn't handle non-finite values.
Results may differ from the reference program's by a relative error of at most 0.023.
Values may be sent and summed in bfloat16 or wider, within the bound.
A program may use at most 128 MiB of HBM per device.

```python
import jax
import jax.numpy as jnp
from jax import lax

TILE_T = 3
TILE_H = 8
TILE_W = 8
TILE_W_DEV = 1
HEADS = 12
HEAD_DIM = 128
TEXT = 256
TILE_TOKENS = 192
FRAMES = 24
HEIGHT = 16
WIDTH = 32
CHANNELS = 1536


def base_field(key):
    noise = jax.random.normal(jax.random.fold_in(key, 7), (FRAMES, HEIGHT, WIDTH, HEADS, HEAD_DIM), jnp.float32)
    return jnp.clip(noise, -6.0, 6.0)


def draw_query(key, part):
    shared = base_field(key)
    key = jax.random.fold_in(key, 3)
    result = jnp.clip(jax.random.normal(key, shared.shape, jnp.float32), -6.0, 6.0)
    return result.reshape(FRAMES, HEIGHT, WIDTH, HEADS * HEAD_DIM).astype(jnp.bfloat16)


def draw_keys(key, part):
    shared = base_field(key)
    result = shared
    return result.reshape(FRAMES, HEIGHT, WIDTH, HEADS * HEAD_DIM).astype(jnp.bfloat16)


def draw_window(key, part):
    key = jax.random.fold_in(key, 5)
    reaches = jax.random.randint(jax.random.fold_in(key, 1), (HEADS, 3), 0, 2, dtype=jnp.int32)
    chosen = jax.random.randint(jax.random.fold_in(key, 2), (), 0, HEADS, dtype=jnp.int32)
    picked = (jnp.arange(HEADS, dtype=jnp.int32) == chosen)[:, None]
    return jnp.where(picked, 1, reaches).astype(jnp.int32)


def levels(stream_key, dims, pieces, low, top_value):
    factor_of, own = 1.0, jax.random.fold_in(stream_key, 6)
    for axis_at, shards_of in pieces:
        draws = jnp.exp(jax.random.uniform(jax.random.fold_in(own, axis_at), (shards_of,), jnp.float32, low / len(pieces), top_value / len(pieces)))
        factor_of = factor_of * jnp.repeat(draws, dims[axis_at] // shards_of).reshape([-1 if axis == axis_at else 1 for axis in range(len(dims))])
    return factor_of


def scatter_about(rng, shape, scale, reach, pieces=(), held_as=jnp.bfloat16):
    values = scale * jax.random.normal(rng, shape, jnp.float32)
    if pieces:
        values = values * levels(rng, shape, pieces, -0.22, 0.18)
    return jnp.clip(values, -reach, reach).astype(held_as)


def setup_inputs(seed: int = 0) -> dict:
    key_of = jax.random.split(jax.random.key(seed), 8)
    return {
        "query": draw_query(jax.random.fold_in(key_of[7], 71), 0),
        "keys": draw_keys(jax.random.fold_in(key_of[7], 71), 0),
        "values": scatter_about(key_of[2], (FRAMES, HEIGHT, WIDTH, CHANNELS), 1.0, 6.0, ((0, 8), (1, 2), (2, 4), (3, 4))),
        "grad_out": scatter_about(key_of[3], (FRAMES, HEIGHT, WIDTH, CHANNELS), 1.0, 6.0, ((0, 8), (1, 2), (2, 4), (3, 4))),
        "text_keys": scatter_about(key_of[4], (TEXT, CHANNELS), 1.0, 6.0, ((1, 4),)),
        "text_values": scatter_about(key_of[5], (TEXT, CHANNELS), 1.0, 6.0, ((1, 4),)),
        "window": draw_window(jax.random.fold_in(key_of[7], 71), 0),
    }


def tile_view(field):
    n_time = FRAMES // TILE_T
    n_rows = HEIGHT // TILE_H
    n_cols = WIDTH // TILE_W
    shaped = field.reshape(n_time, TILE_T, n_rows, TILE_H, n_cols, TILE_W, CHANNELS)
    shaped = shaped.transpose(0, 2, 4, 1, 3, 5, 6)
    return shaped.reshape(n_time, n_rows, n_cols, TILE_TOKENS, HEADS, HEAD_DIM)


def grid_view(tiles):
    n_time = FRAMES // TILE_T
    n_rows = HEIGHT // TILE_H
    n_cols = WIDTH // TILE_W
    shaped = tiles.reshape(n_time, n_rows, n_cols, TILE_T, TILE_H, TILE_W, CHANNELS)
    shaped = shaped.transpose(0, 3, 1, 4, 2, 5, 6)
    return shaped.reshape(FRAMES, HEIGHT, WIDTH, CHANNELS)


def reference(query, keys, values, grad_out, text_keys, text_values, window):
    n_time = FRAMES // TILE_T
    n_rows = HEIGHT // TILE_H
    n_cols = WIDTH // TILE_W
    scaling = HEAD_DIM ** -0.5
    f32 = jnp.float32
    query_tiles = tile_view(query)
    key_tiles = tile_view(keys)
    value_tiles = tile_view(values)
    grad_tiles = tile_view(grad_out)
    padding = ((1, 1), (1, 1), (1, 1), (0, 0), (0, 0), (0, 0))
    key_padded = jnp.pad(key_tiles, padding)
    value_padded = jnp.pad(value_tiles, padding)
    query_padded = jnp.pad(query_tiles, padding)
    grad_padded = jnp.pad(grad_tiles, padding)
    text_key = text_keys.reshape(TEXT, HEADS, HEAD_DIM).astype(f32)
    text_value = text_values.reshape(TEXT, HEADS, HEAD_DIM).astype(f32)
    offsets = jnp.arange(3, dtype=jnp.int32) - 1
    anchor = jnp.zeros((), jnp.int32)

    def axis_reach(place, count, column_of):
        spot = place + offsets
        inside = (spot >= 0) & (spot < count)
        return (jnp.abs(offsets)[None, :] <= window[:, column_of:column_of + 1]) & inside[None, :]

    def tile_mask(slab_t, slab_h, slab_w):
        in_time = axis_reach(slab_t, n_time, 0)
        in_rows = axis_reach(slab_h, n_rows, 1)
        in_cols = axis_reach(slab_w, n_cols, 2)
        return in_time[:, :, None, None] & in_rows[:, None, :, None] & in_cols[:, None, None, :]

    def split_index(tile_index):
        slab_t = (tile_index // (n_rows * n_cols)).astype(jnp.int32)
        slab_h = ((tile_index // n_cols) % n_rows).astype(jnp.int32)
        slab_w = (tile_index % n_cols).astype(jnp.int32)
        return slab_t, slab_h, slab_w

    def own_tile(tiles, slab_t, slab_h, slab_w):
        piece = lax.dynamic_slice(tiles, (slab_t, slab_h, slab_w, anchor, anchor, anchor), (1, 1, 1, TILE_TOKENS, HEADS, HEAD_DIM))
        return piece.reshape(TILE_TOKENS, HEADS, HEAD_DIM)

    def near_tiles(padded, slab_t, slab_h, slab_w):
        return lax.dynamic_slice(padded, (slab_t, slab_h, slab_w, anchor, anchor, anchor), (3, 3, 3) + padded.shape[3:])

    def forward_tile(tile_index):
        slab_t, slab_h, slab_w = split_index(tile_index)
        query_tile = own_tile(query_tiles, slab_t, slab_h, slab_w).astype(f32)
        grad_tile = own_tile(grad_tiles, slab_t, slab_h, slab_w).astype(f32)
        region_key = near_tiles(key_padded, slab_t, slab_h, slab_w).reshape(27 * TILE_TOKENS, HEADS, HEAD_DIM).astype(f32)
        region_value = near_tiles(value_padded, slab_t, slab_h, slab_w).reshape(27 * TILE_TOKENS, HEADS, HEAD_DIM).astype(f32)
        all_keys = jnp.concatenate([text_key, region_key], 0)
        all_values = jnp.concatenate([text_value, region_value], 0)
        latent_mask = jnp.broadcast_to(tile_mask(slab_t, slab_h, slab_w)[..., None], (HEADS, 3, 3, 3, TILE_TOKENS)).reshape(HEADS, 27 * TILE_TOKENS)
        allowed = jnp.concatenate([jnp.ones((HEADS, TEXT), bool), latent_mask], 1)
        scores = jnp.einsum('qhd,khd->hqk', query_tile, all_keys) * scaling
        scores = jnp.where(allowed[:, None, :], scores, -jnp.inf)
        row_peak = jnp.max(scores, axis=-1, keepdims=True)
        log_norm = row_peak + jnp.log(jnp.sum(jnp.exp(scores - row_peak), axis=-1, keepdims=True))
        weights = jnp.exp(scores - log_norm).astype(jnp.bfloat16).astype(f32)
        out_tile = jnp.einsum('hqk,khd->qhd', weights, all_values).astype(jnp.bfloat16)
        out_dot = jnp.sum(grad_tile * out_tile.astype(f32), axis=-1).T
        prob_grad = jnp.einsum('qhd,khd->hqk', grad_tile, all_values)
        score_grad = (weights * (prob_grad - out_dot[:, :, None])).astype(jnp.bfloat16).astype(f32)
        query_grad = (scaling * jnp.einsum('hqk,khd->qhd', score_grad, all_keys)).astype(jnp.bfloat16)
        text_kpart = scaling * jnp.einsum('hqk,qhd->khd', score_grad[:, :, :TEXT], query_tile)
        text_vpart = jnp.einsum('hqk,qhd->khd', weights[:, :, :TEXT], grad_tile)
        return out_tile, query_grad, log_norm[..., 0], out_dot, text_kpart, text_vpart

    tile_ids = jnp.arange(n_time * n_rows * n_cols, dtype=jnp.int32)
    out_list, dq_list, norm_list, dot_list, text_kparts, text_vparts = lax.map(forward_tile, tile_ids)
    grid_shape = (n_time, n_rows, n_cols)
    norm_padded = jnp.pad(norm_list.reshape(grid_shape + (HEADS, TILE_TOKENS)), padding[:5])
    dot_padded = jnp.pad(dot_list.reshape(grid_shape + (HEADS, TILE_TOKENS)), padding[:5])

    def key_tile(tile_index):
        slab_t, slab_h, slab_w = split_index(tile_index)
        key_own = own_tile(key_tiles, slab_t, slab_h, slab_w).astype(f32)
        value_own = own_tile(value_tiles, slab_t, slab_h, slab_w).astype(f32)
        near_query = near_tiles(query_padded, slab_t, slab_h, slab_w).astype(f32)
        near_grad = near_tiles(grad_padded, slab_t, slab_h, slab_w).astype(f32)
        near_norm = lax.dynamic_slice(norm_padded, (slab_t, slab_h, slab_w, anchor, anchor), (3, 3, 3, HEADS, TILE_TOKENS))
        near_dot = lax.dynamic_slice(dot_padded, (slab_t, slab_h, slab_w, anchor, anchor), (3, 3, 3, HEADS, TILE_TOKENS))
        allowed = tile_mask(slab_t, slab_h, slab_w).transpose(1, 2, 3, 0)
        scores = jnp.einsum('tuvqhd,khd->tuvhqk', near_query, key_own) * scaling
        weights = jnp.where(allowed[..., None, None], jnp.exp(scores - near_norm[..., None]), 0.0)
        weights = weights.astype(jnp.bfloat16).astype(f32)
        prob_grad = jnp.einsum('tuvqhd,khd->tuvhqk', near_grad, value_own)
        score_grad = (weights * (prob_grad - near_dot[..., None])).astype(jnp.bfloat16).astype(f32)
        key_parts = scaling * jnp.einsum('tuvhqk,tuvqhd->tuvkhd', score_grad, near_query)
        value_parts = jnp.einsum('tuvhqk,tuvqhd->tuvkhd', weights, near_grad)
        block_ids = jnp.floor_divide(slab_w + offsets, TILE_W_DEV)
        shared_block = (block_ids[:, None] == block_ids[None, :]).astype(f32)
        leading = (jnp.sum(jnp.tril(shared_block, -1), axis=1) == 0).astype(f32)

        def settle(parts):
            grouped = jnp.einsum('ij,tujkhd->tuikhd', shared_block, parts, precision=lax.Precision.HIGHEST)
            rounded = lax.optimization_barrier(grouped.astype(jnp.bfloat16)).astype(f32)
            return jnp.sum(rounded * leading[None, None, :, None, None, None], axis=(0, 1, 2)).astype(jnp.bfloat16)

        return settle(key_parts), settle(value_parts)

    key_list, value_list = lax.map(key_tile, tile_ids)
    tile_shape = grid_shape + (TILE_TOKENS, HEADS, HEAD_DIM)
    out = grid_view(out_list.reshape(tile_shape))
    query_grad = grid_view(dq_list.reshape(tile_shape))
    key_grad = grid_view(key_list.reshape(tile_shape))
    value_grad = grid_view(value_list.reshape(tile_shape))
    text_key_grad = jnp.sum(text_kparts, axis=0).reshape(TEXT, CHANNELS).astype(jnp.bfloat16)
    text_value_grad = jnp.sum(text_vparts, axis=0).reshape(TEXT, CHANNELS).astype(jnp.bfloat16)
    return out, query_grad, key_grad, value_grad, text_key_grad, text_value_grad
```

```python
import functools

import jax
import jax.numpy as jnp
from jax import lax
from jax.experimental import pallas as pl
from jax.experimental.pallas import tpu as pltpu
from jax.sharding import PartitionSpec as P

MESH = pl.DeviceIdType.MESH
MASKED = -1e30
LOG2E = 1.4426950408889634
KEY, VALUE, QUERY, GRAD = 0, 1, 2, 3


def nt_dot(a, b):
    return lax.dot_general(a, b, (((1,), (1,)), ((), ())), preferred_element_type=jnp.float32)


def nn_dot(a, b):
    return jnp.dot(a, b, preferred_element_type=jnp.float32)


def kernel(
    sizes,
    keys_ref, values_ref, query_ref, grad_ref, text_key_ref, text_value_ref, window_ref,
    out_ref, dq_ref, dk_ref, dv_ref, dtk_ref, dtv_ref,
    slots, scores, text_scores, probs, text_probs, weights, text_weights,
    bias, peak, stats, dk_acc, dv_acc,
    text_send, text_recv, sum_send, sum_recv,
    load_sem, up_send, down_send, side_send, slot_recv, stat_send, stat_recv,
    part_send, part_recv, total_send, total_recv,
):
    n_time, n_rows, n_cols, heads, head_dim, tokens, n_text = sizes
    f32, bf16 = jnp.float32, jnp.bfloat16
    scale = head_dim ** -0.5
    factor = scale * LOG2E
    n_z = n_rows * n_cols
    rows_time = n_text // n_time
    rows_dev = rows_time // n_z
    pair = 2 * tokens

    t = lax.axis_index("ta")
    h = lax.axis_index("ha")
    w = lax.axis_index("wa")
    z = n_rows * w + h
    base = n_rows * (w - 1)
    mine = 6 + 2 + h

    def z_device(at):
        return {"ha": lax.rem(at, n_rows), "wa": lax.div(at, n_rows)}

    def in_z(at):
        return (at >= 0) & (at < n_z)

    def in_t(at):
        return (at >= 0) & (at < n_time)

    def lanes(head):
        return slice(head * head_dim, (head + 1) * head_dim)

    loads = [
        pltpu.make_async_copy(ref, slots.at[array, mine], load_sem.at[array])
        for array, ref in ((KEY, keys_ref), (VALUE, values_ref), (QUERY, query_ref), (GRAD, grad_ref))
    ]
    for load in loads:
        load.start()

    barrier = pltpu.get_barrier_semaphore()
    for step in range(1, n_time):
        pl.semaphore_signal(barrier, 1, device_id={"ta": lax.rem(t + step, n_time)}, device_id_type=MESH)
    for step in range(1, n_z):
        pl.semaphore_signal(barrier, 1, device_id=z_device(lax.rem(z + step, n_z)), device_id_type=MESH)
    for away in (-1, 1):
        for spot in range(6):
            there = base + spot

            @pl.when(in_t(t + away) & in_z(there) & (spot != 2 + h))
            def _():
                pl.semaphore_signal(
                    barrier, 1, device_id={"ta": t + away, **z_device(there)}, device_id_type=MESH
                )

    def zero_slot(index, carry):
        time_at, z_at = t + lax.div(index, 6) - 1, base + lax.rem(index, 6)

        @pl.when(jnp.logical_not(in_t(time_at) & in_z(z_at)))
        def _():
            for array in range(4):
                slots[array, index] = jnp.zeros((tokens, heads * head_dim), bf16)
            stats[index] = jnp.zeros((8, pair), f32)

        return carry

    lax.fori_loop(0, 18, zero_slot, 0)

    lane = lax.broadcasted_iota(jnp.int32, (1, pair), 1)
    for head in range(heads):
        reach_t, reach_h, reach_w = (window_ref[head, axis] for axis in range(3))
        for dt in range(3):
            for block in range(3):
                near = (
                    in_t(t + dt - 1)
                    & (w + block - 1 >= 0)
                    & (w + block - 1 < n_cols)
                    & (abs(dt - 1) <= reach_t)
                    & (abs(block - 1) <= reach_w)
                )
                open_low = near & (h <= reach_h)
                open_high = near & (1 - h <= reach_h)
                low = jnp.where(open_low, 0.0, MASKED).astype(f32)
                high = jnp.where(open_high, 0.0, MASKED).astype(f32)
                bias[head * 9 + dt * 3 + block] = jnp.where(lane < tokens, low, high)

    n_near = in_t(t - 1).astype(jnp.int32) + in_t(t + 1).astype(jnp.int32)
    n_line = in_z(base).astype(jnp.int32) * 2 + in_z(base + 4).astype(jnp.int32) * 2 + 1
    pl.semaphore_wait(barrier, n_time - 1 + n_z - 1 + n_near * n_line)

    def z_copy(array, step, way):
        tile = z - way * step
        there = z + way
        there_base = n_rows * (lax.div(there + n_rows, n_rows) - 2)
        sems = up_send if way == 1 else down_send
        dst = 6 + tile - there_base
        return pltpu.make_async_remote_copy(
            src_ref=slots.at[array, 6 + tile - base],
            dst_ref=slots.at[array, dst],
            send_sem=sems.at[array, step],
            recv_sem=slot_recv.at[array, dst],
            device_id=z_device(there),
            device_id_type=MESH,
        )

    def z_wanted(step, way):
        ok = in_z(z + way) & in_z(z - way * step)
        if step == 2:
            ok = ok & (h == (0 if way == 1 else 1))
        return ok

    def t_copy(array, spot, way):
        dst = 6 - 6 * way + spot
        return pltpu.make_async_remote_copy(
            src_ref=slots.at[array, 6 + spot],
            dst_ref=slots.at[array, dst],
            send_sem=side_send.at[array, (way + 1) // 2, spot],
            recv_sem=slot_recv.at[array, dst],
            device_id={"ta": t + way},
            device_id_type=MESH,
        )

    def wait_slot(array, slot):
        pltpu.make_async_copy(slots.at[array, slot], slots.at[array, slot], slot_recv.at[array, slot]).wait()

    def send_z(array, step, way):
        @pl.when(z_wanted(step, way))
        def _():
            z_copy(array, step, way).start()

    def send_t(array, spot):
        for way in (1, -1):
            @pl.when(in_t(t + way))
            def _():
                t_copy(array, spot, way).start()

    def send_own(array):
        send_z(array, 0, 1)
        send_z(array, 0, -1)
        send_t(array, 2 + h)

    def arrive(array, step):
        for way in (1, -1):
            tile = z - way * step
            ok = in_z(tile)
            if step == 3:
                ok = ok & (h == (1 if way == 1 else 0))

            @pl.when(ok)
            def _():
                wait_slot(array, 6 + tile - base)
                if step < 3:
                    send_z(array, step, way)
                send_t(array, tile - base)

    def await_pair(arrays, dt, block):
        for spot in (2 * block, 2 * block + 1):
            @pl.when(in_t(t + dt - 1) & in_z(base + spot))
            def _():
                for array in arrays:
                    wait_slot(array, 6 * dt + spot)

    def stat_copy(away, spot):
        there = base + spot
        dst = 6 - 6 * away + h + 4 - 2 * (spot // 2)
        return pltpu.make_async_remote_copy(
            src_ref=stats.at[mine],
            dst_ref=stats.at[dst],
            send_sem=stat_send.at[6 * (away + 1) + spot],
            recv_sem=stat_recv.at[dst],
            device_id={"ta": t + away, **z_device(there)},
            device_id_type=MESH,
        )

    def stat_wanted(away, spot):
        ok = in_t(t + away) & in_z(base + spot)
        if away == 0 and spot in (2, 3):
            ok = ok & (spot != 2 + h)
        return ok

    def await_stats(dt, block):
        for spot in (2 * block, 2 * block + 1):
            @pl.when(in_t(t + dt - 1) & in_z(base + spot) & (6 * dt + spot != mine))
            def _():
                slot = 6 * dt + spot
                pltpu.make_async_copy(stats.at[slot], stats.at[slot], stat_recv.at[slot]).wait()

    def pair_of(array, j, head):
        return slots[array, pl.ds(2 * j, 2), :, lanes(head)].reshape(pair, head_dim)

    def forward_pair(j):
        for head in range(heads):
            q = slots[QUERY, mine, :, lanes(head)]
            g = slots[GRAD, mine, :, lanes(head)]
            s = nt_dot(q, pair_of(KEY, j, head)) + bias[head * 9 + j]
            scores[head * 9 + j] = s
            top = peak[head]
            for at in range(0, pair, 128):
                top = jnp.maximum(top, s[:, at : at + 128])
            peak[head] = top
            probs[head * 9 + j] = nt_dot(g, pair_of(VALUE, j, head))

    def backward_pair(j):
        both = stats[2 * j] + stats[2 * j + 1]
        for head in range(heads):
            norm = both[head : head + 1] - bias[head * 9 + j]
            dot = both[heads + head : heads + head + 1]
            q = pair_of(QUERY, j, head)
            g = pair_of(GRAD, j, head)
            s = nt_dot(slots[KEY, mine, :, lanes(head)], q)
            p = jnp.exp2(s * factor - norm)
            d = nt_dot(slots[VALUE, mine, :, lanes(head)], g)
            ds = (p * (d - dot)).astype(bf16)
            dv_acc[:, lanes(head)] += nn_dot(p.astype(bf16), g)
            dk_acc[:, lanes(head)] += nn_dot(ds, q)

    def both_times(work, block):
        def body(index, carry):
            work(2 * index, block)
            return carry

        lax.fori_loop(0, 2, body, 0)

    def forward_side(dt, block):
        await_pair((KEY, VALUE), dt, block)
        forward_pair(3 * dt + block)

    def backward_side(dt, block):
        await_pair((QUERY, GRAD), dt, block)
        await_stats(dt, block)
        backward_pair(3 * dt + block)

    near, far = 2 * h, 2 - 2 * h

    loads[KEY].wait()
    send_own(KEY)
    loads[VALUE].wait()
    send_own(VALUE)
    loads[QUERY].wait()
    loads[GRAD].wait()

    for head in range(heads):
        q = slots[QUERY, mine, :, lanes(head)]
        g = slots[GRAD, mine, :, lanes(head)]
        s = nt_dot(q, text_key_ref[:, lanes(head)])
        text_scores[head] = s
        top = s[:, :128]
        for at in range(128, n_text, 128):
            top = jnp.maximum(top, s[:, at : at + 128])
        peak[head] = top
        text_probs[head] = nt_dot(g, text_value_ref[:, lanes(head)])
    dk_acc[...] = jnp.zeros_like(dk_acc)
    dv_acc[...] = jnp.zeros_like(dv_acc)

    arrive(KEY, 1)
    arrive(VALUE, 1)
    forward_pair(4)
    arrive(KEY, 2)
    arrive(VALUE, 2)
    send_own(QUERY)
    send_own(GRAD)
    both_times(forward_side, 1)
    forward_pair(3 + near)
    arrive(KEY, 3)
    arrive(VALUE, 3)
    forward_pair(3 + far)
    both_times(forward_side, near)
    both_times(forward_side, far)
    arrive(QUERY, 1)

    row_lane = lax.broadcasted_iota(jnp.int32, (tokens, 128), 1)
    columns = jnp.zeros((tokens, 128), f32)
    inverse, dots = [], []
    for head in range(heads):
        top = jnp.max(peak[head], axis=1, keepdims=True) * factor
        p = jnp.exp2(text_scores[head] * factor - top)
        total = p[:, :128]
        for at in range(128, n_text, 128):
            total = total + p[:, at : at + 128]
        p = p.astype(bf16)
        text_weights[head] = p
        acc = nn_dot(p, text_value_ref[:, lanes(head)])

        def weigh(j, carry, head=head, top=top):
            total, acc = carry
            p = jnp.exp2(scores[head * 9 + j] * factor - top)
            for at in range(0, pair, 128):
                total = total + p[:, at : at + 128]
            p = p.astype(bf16)
            weights[head * 9 + j] = p
            return total, acc + nn_dot(p, pair_of(VALUE, j, head))

        total, acc = lax.fori_loop(0, 9, weigh, (total, acc))
        total = jnp.sum(total, axis=1, keepdims=True)
        inv = 1.0 / total
        out = (acc * inv).astype(bf16)
        out_ref[:, lanes(head)] = out
        g = slots[GRAD, mine, :, lanes(head)].astype(f32)
        dot = jnp.sum(g * out.astype(f32), axis=1, keepdims=True)
        inverse.append(inv)
        dots.append(dot)
        columns = jnp.where(row_lane == head, top + jnp.log2(total), columns)
        columns = jnp.where(row_lane == heads + head, dot, columns)

    own_stats = jnp.transpose(columns)[:8]
    blank = jnp.zeros((8, tokens), f32)
    stats[mine] = jnp.where(
        h == 0,
        jnp.concatenate([own_stats, blank], axis=1),
        jnp.concatenate([blank, own_stats], axis=1),
    )
    for away in (-1, 0, 1):
        for spot in range(6):
            @pl.when(stat_wanted(away, spot))
            def _():
                stat_copy(away, spot).start()
    arrive(GRAD, 1)

    for head in range(heads):
        q = slots[QUERY, mine, :, lanes(head)]
        g = slots[GRAD, mine, :, lanes(head)]
        p = jnp.exp2(nt_dot(text_key_ref[:, lanes(head)], q) * factor - own_stats[head : head + 1])
        d = nt_dot(text_value_ref[:, lanes(head)], g)
        ds = (p * (d - own_stats[heads + head : heads + head + 1])).astype(bf16)
        dtv = nn_dot(p.astype(bf16), g).astype(bf16)
        dtk = (nn_dot(ds, q) * scale).astype(bf16)
        for part in range(n_time):
            rows = slice(part * rows_time, (part + 1) * rows_time)
            text_send[part, 0, :, lanes(head)] = dtk[rows]
            text_send[part, 1, :, lanes(head)] = dtv[rows]

    def part_copy(step):
        there = lax.rem(t + step, n_time)
        return pltpu.make_async_remote_copy(
            src_ref=text_send.at[there],
            dst_ref=text_recv.at[t],
            send_sem=part_send.at[step],
            recv_sem=part_recv.at[t],
            device_id={"ta": there},
            device_id_type=MESH,
        )

    for step in range(1, n_time):
        part_copy(step).start()
    text_recv[t] = text_send[t]

    arrive(QUERY, 2)

    for head in range(heads):
        dot = dots[head]
        ds = (text_weights[head].astype(f32) * (text_probs[head] - dot)).astype(bf16)
        acc = nn_dot(ds, text_key_ref[:, lanes(head)])

        def pull(j, acc, head=head, dot=dot):
            ds = (weights[head * 9 + j].astype(f32) * (probs[head * 9 + j] - dot)).astype(bf16)
            return acc + nn_dot(ds, pair_of(KEY, j, head))

        acc = lax.fori_loop(0, 9, pull, acc)
        dq_ref[:, lanes(head)] = (acc * (inverse[head] * scale)).astype(bf16)

    arrive(GRAD, 2)

    await_stats(1, 1)
    backward_pair(4)
    both_times(backward_side, 1)

    for step in range(1, n_time):
        src = lax.rem(t + step, n_time)
        pltpu.make_async_copy(text_recv.at[src], text_recv.at[src], part_recv.at[src]).wait()
    summed = text_recv[0].astype(f32)
    for src in range(1, n_time):
        summed = summed + text_recv[src].astype(f32)
    for part in range(n_z):
        rows = slice(part * rows_dev, (part + 1) * rows_dev)
        sum_send[part, 0:rows_dev] = summed[0, rows]
        sum_send[part, rows_dev : 2 * rows_dev] = summed[1, rows]

    def total_copy(step):
        there = lax.rem(z + step, n_z)
        to_h, to_w = lax.rem(there, n_rows), lax.div(there, n_rows)
        return pltpu.make_async_remote_copy(
            src_ref=sum_send.at[to_h * n_cols + to_w],
            dst_ref=sum_recv.at[z],
            send_sem=total_send.at[step],
            recv_sem=total_recv.at[z],
            device_id=z_device(there),
            device_id_type=MESH,
        )

    for step in range(1, n_z):
        total_copy(step).start()
    sum_recv[z] = sum_send[h * n_cols + w]

    await_stats(1, near)
    backward_pair(3 + near)
    arrive(QUERY, 3)
    arrive(GRAD, 3)
    await_stats(1, far)
    backward_pair(3 + far)
    both_times(backward_side, near)
    both_times(backward_side, far)

    dk_ref[...] = (dk_acc[...] * scale).astype(bf16)
    dv_ref[...] = dv_acc[...].astype(bf16)

    for step in range(1, n_z):
        src = lax.rem(z + step, n_z)
        pltpu.make_async_copy(sum_recv.at[src], sum_recv.at[src], total_recv.at[src]).wait()
    final = sum_recv[0]
    for src in range(1, n_z):
        final = final + sum_recv[src]
    dtk_ref[...] = final[0:rows_dev].astype(bf16)
    dtv_ref[...] = final[rows_dev : 2 * rows_dev].astype(bf16)

    for array in range(4):
        for way in (1, -1):
            for step in range(3):
                @pl.when(z_wanted(step, way))
                def _():
                    z_copy(array, step, way).wait_send()

            for spot in range(6):
                @pl.when(in_t(t + way) & in_z(base + spot))
                def _():
                    t_copy(array, spot, way).wait_send()

    for away in (-1, 0, 1):
        for spot in range(6):
            @pl.when(stat_wanted(away, spot))
            def _():
                stat_copy(away, spot).wait_send()

    for step in range(1, n_time):
        part_copy(step).wait_send()
    for step in range(1, n_z):
        total_copy(step).wait_send()


def on_device(query, keys, values, grad_out, text_keys, text_values, window):
    bf16, f32 = jnp.bfloat16, jnp.float32
    frames, height, wide, chans = query.shape
    heads = window.shape[0]
    head_dim = chans // heads
    tokens = frames * height * wide
    n_text = text_keys.shape[0]
    n_time, n_rows, n_cols = (lax.axis_size(axis) for axis in ("ta", "ha", "wa"))
    n_z = n_rows * n_cols
    rows_time = n_text // n_time
    rows_dev = rows_time // n_z
    sizes = (n_time, n_rows, n_cols, heads, head_dim, tokens, n_text)
    pair = 2 * tokens
    tile = jax.ShapeDtypeStruct((tokens, chans), bf16)
    text = jax.ShapeDtypeStruct((rows_dev, chans), bf16)
    anywhere = pl.BlockSpec(memory_space=pl.ANY)
    vmem = pl.BlockSpec(memory_space=pltpu.VMEM)
    smem = pl.BlockSpec(memory_space=pltpu.SMEM)
    dma = pltpu.SemaphoreType.DMA
    flat = [array.reshape(tokens, chans) for array in (keys, values, query, grad_out)]
    out, dq, dk, dv, dtk, dtv = pl.pallas_call(
        functools.partial(kernel, sizes),
        out_shape=(tile, tile, tile, tile, text, text),
        in_specs=[anywhere] * 4 + [vmem] * 2 + [smem],
        out_specs=(vmem,) * 6,
        scratch_shapes=[
            pltpu.VMEM((4, 18, tokens, chans), bf16),
            pltpu.VMEM((9 * heads, tokens, pair), f32),
            pltpu.VMEM((heads, tokens, n_text), f32),
            pltpu.VMEM((9 * heads, tokens, pair), f32),
            pltpu.VMEM((heads, tokens, n_text), f32),
            pltpu.VMEM((9 * heads, tokens, pair), bf16),
            pltpu.VMEM((heads, tokens, n_text), bf16),
            pltpu.VMEM((9 * heads, 1, pair), f32),
            pltpu.VMEM((heads, tokens, 128), f32),
            pltpu.VMEM((18, 8, pair), f32),
            pltpu.VMEM((tokens, chans), f32),
            pltpu.VMEM((tokens, chans), f32),
            pltpu.VMEM((n_time, 2, rows_time, chans), bf16),
            pltpu.VMEM((n_time, 2, rows_time, chans), bf16),
            pltpu.VMEM((n_z, 2 * rows_dev, chans), f32),
            pltpu.VMEM((n_z, 2 * rows_dev, chans), f32),
            dma((4,)),
            dma((4, 3)),
            dma((4, 3)),
            dma((4, 2, 6)),
            dma((4, 18)),
            dma((18,)),
            dma((18,)),
            dma((n_time,)),
            dma((n_time,)),
            dma((n_z,)),
            dma((n_z,)),
        ],
        compiler_params=pltpu.CompilerParams(
            collective_id=0, has_side_effects=True, vmem_limit_bytes=56 * 1024 * 1024
        ),
    )(*flat, text_keys, text_values, window)
    shape = (frames, height, wide, chans)
    return tuple(array.reshape(shape) for array in (out, dq, dk, dv)) + (dtk, dtv)


def solution(mesh):
    tiled = P("ta", "ha", "wa", "head")
    placed = (tiled, tiled, tiled, tiled, P(None, "head"), P(None, "head"), P("head", None))
    text = P(("ta", "ha", "wa"), "head")
    return jax.shard_map(
        on_device,
        mesh=mesh,
        in_specs=placed,
        out_specs=(tiled, tiled, tiled, tiled, text, text),
        check_vma=False,
    )
```

```python
import functools

import jax
import jax.numpy as jnp
from jax import lax
from jax.experimental import pallas as pl
from jax.experimental.pallas import tpu as pltpu
from jax.sharding import PartitionSpec as P

MESH = pl.DeviceIdType.MESH
MASKED = -1e30
LOG2E = 1.4426950408889634
KEY, VALUE, QUERY, GRAD = 0, 1, 2, 3


def nt_dot(a, b):
    return lax.dot_general(a, b, (((1,), (1,)), ((), ())), preferred_element_type=jnp.float32)


def nn_dot(a, b):
    return jnp.dot(a, b, preferred_element_type=jnp.float32)


def kernel(
    sizes,
    keys_ref, values_ref, query_ref, grad_ref, text_key_in, text_value_in, window_ref,
    out_ref, dq_ref, dk_ref, dv_ref, dtk_ref, dtv_ref,
    slots, text, scores, text_scores, probs, text_probs, weights, text_weights,
    bias, peak, stats, dk_acc, dv_acc,
    text_send, text_near, text_far, text_recv, sum_send, sum_recv,
    load_sem, up_send, down_send, side_send, slot_recv, stat_send, stat_recv,
    core_recv, part_send, part_recv, total_send, total_recv,
):
    n_time, n_rows, n_cols, heads, head_dim, tokens, n_text = sizes
    f32, bf16 = jnp.float32, jnp.bfloat16
    scale = head_dim ** -0.5
    factor = scale * LOG2E
    n_z = n_rows * n_cols
    rows_time = n_text // n_time
    rows_dev = rows_time // n_z
    pair = 2 * tokens

    t = lax.axis_index("ta")
    h = lax.axis_index("ha")
    w = lax.axis_index("wa")
    z = n_rows * w + h
    base = n_rows * (w - 1)
    mine = 6 + 2 + h

    def z_device(at):
        return {"ha": lax.rem(at, n_rows), "wa": lax.div(at, n_rows)}

    def in_z(at):
        return (at >= 0) & (at < n_z)

    def in_t(at):
        return (at >= 0) & (at < n_time)

    def lanes(head):
        return slice(head * head_dim, (head + 1) * head_dim)

    loads = [
        pltpu.make_async_copy(ref, slots.at[array, mine], load_sem.at[array])
        for array, ref in ((KEY, keys_ref), (VALUE, values_ref), (QUERY, query_ref), (GRAD, grad_ref))
    ]
    loads += [
        pltpu.make_async_copy(ref, text.at[at], load_sem.at[4 + at])
        for at, ref in enumerate((text_key_in, text_value_in))
    ]
    for load in loads:
        load.start()

    barrier = pltpu.get_barrier_semaphore()
    for step in range(1, n_time):
        pl.semaphore_signal(barrier, 1, device_id={"ta": lax.rem(t + step, n_time)}, device_id_type=MESH)
    for step in range(1, n_z):
        pl.semaphore_signal(barrier, 1, device_id=z_device(lax.rem(z + step, n_z)), device_id_type=MESH)
    pl.semaphore_wait(barrier, n_time - 1 + n_z - 1)

    def z_copy(array, step, way):
        tile = z - way * step
        there = z + way
        there_base = n_rows * (lax.div(there + n_rows, n_rows) - 2)
        sems = up_send if way == 1 else down_send
        dst = 6 + tile - there_base
        return pltpu.make_async_remote_copy(
            src_ref=slots.at[array, 6 + tile - base],
            dst_ref=slots.at[array, dst],
            send_sem=sems.at[array, step],
            recv_sem=slot_recv.at[array, dst],
            device_id=z_device(there),
            device_id_type=MESH,
        )

    def z_wanted(step, way):
        ok = in_z(z + way) & in_z(z - way * step)
        if step == 2:
            ok = ok & (h == (0 if way == 1 else 1))
        return ok

    def t_copy(array, spot, way):
        dst = 6 - 6 * way + spot
        return pltpu.make_async_remote_copy(
            src_ref=slots.at[array, 6 + spot],
            dst_ref=slots.at[array, dst],
            send_sem=side_send.at[array, (way + 1) // 2, spot],
            recv_sem=slot_recv.at[array, dst],
            device_id={"ta": t + way},
            device_id_type=MESH,
        )

    def wait_slot(array, slot):
        pltpu.make_async_copy(slots.at[array, slot], slots.at[array, slot], slot_recv.at[array, slot]).wait()

    def send_z(array, step, way):
        @pl.when(z_wanted(step, way))
        def _():
            z_copy(array, step, way).start()

    def send_t(array, spot):
        for way in (1, -1):
            @pl.when(in_t(t + way))
            def _():
                t_copy(array, spot, way).start()

    def send_own(array):
        send_z(array, 0, 1)
        send_z(array, 0, -1)

    def settle(array):
        for way in (1, -1):
            for step in range(3):
                @pl.when(z_wanted(step, way))
                def _():
                    z_copy(array, step, way).wait_send()

            for spot in range(6):
                @pl.when(in_t(t + way) & in_z(base + spot))
                def _():
                    t_copy(array, spot, way).wait_send()

    def arrive(array, step, sides=(0, 1)):
        for side in sides if step < 3 else (1,):
            for way in (1, -1):
                tile = z - way * step
                ok = in_z(tile) & (h == (side if way == 1 else 1 - side))

                @pl.when(ok)
                def _():
                    wait_slot(array, 6 + tile - base)
                    if step < 3:
                        send_z(array, step, way)
                    send_t(array, tile - base)

    def await_pair(arrays, dt, block):
        for spot in (2 * block, 2 * block + 1):
            @pl.when(in_t(t + dt - 1) & in_z(base + spot))
            def _():
                for array in arrays:
                    wait_slot(array, 6 * dt + spot)

    def stat_copy(spot):
        dst = 6 + h + 4 - 2 * (spot // 2)
        return pltpu.make_async_remote_copy(
            src_ref=stats.at[mine],
            dst_ref=stats.at[dst],
            send_sem=stat_send.at[6 + spot],
            recv_sem=stat_recv.at[dst],
            device_id=z_device(base + spot),
            device_id_type=MESH,
        )

    def stat_wanted(spot):
        ok = in_z(base + spot)
        return ok & (spot != 2 + h) if spot in (2, 3) else ok

    def stat_side_copy(spot, way):
        dst = 6 - 6 * way + spot
        return pltpu.make_async_remote_copy(
            src_ref=stats.at[6 + spot],
            dst_ref=stats.at[dst],
            send_sem=stat_send.at[6 + 6 * way + spot],
            recv_sem=stat_recv.at[dst],
            device_id={"ta": t + way},
            device_id_type=MESH,
        )

    def wait_stat(slot):
        pltpu.make_async_copy(stats.at[slot], stats.at[slot], stat_recv.at[slot]).wait()

    def pass_stats(spot):
        for way in (1, -1):
            @pl.when(in_t(t + way))
            def _():
                stat_side_copy(spot, way).start()

    def send_stats():
        for spot in range(6):
            @pl.when(stat_wanted(spot))
            def _():
                stat_copy(spot).start()
        pass_stats(2 + h)

    def arrive_stats():
        for spot in range(6):
            @pl.when(stat_wanted(spot))
            def _():
                wait_stat(6 + spot)
                pass_stats(spot)

    def await_stats(dt, block):
        for spot in (2 * block, 2 * block + 1):
            @pl.when(in_t(t + dt - 1) & in_z(base + spot))
            def _():
                wait_stat(6 * dt + spot)

    def pair_of(array, j, head):
        return slots[array, pl.ds(2 * j, 2), :, lanes(head)].reshape(pair, head_dim)

    def forward_pair(j):
        for head in range(heads):
            q = slots[QUERY, mine, :, lanes(head)]
            g = slots[GRAD, mine, :, lanes(head)]
            s = nt_dot(q, pair_of(KEY, j, head)) + bias[head * 9 + j]
            scores[head * 9 + j] = s
            top = peak[head]
            for at in range(0, pair, 128):
                top = jnp.maximum(top, s[:, at : at + 128])
            peak[head] = top
            probs[head * 9 + j] = nt_dot(g, pair_of(VALUE, j, head))

    def backward_pair(j):
        both = jnp.concatenate([stats[2 * j, :, :tokens], stats[2 * j + 1, :, :tokens]], axis=1)
        for head in range(heads):
            norm = both[head : head + 1] - bias[head * 9 + j]
            dot = both[heads + head : heads + head + 1]
            q = pair_of(QUERY, j, head)
            g = pair_of(GRAD, j, head)
            s = nt_dot(slots[KEY, mine, :, lanes(head)], q)
            p = jnp.exp2(s * factor - norm)
            d = nt_dot(slots[VALUE, mine, :, lanes(head)], g)
            ds = (p * (d - dot)).astype(bf16)
            dv_acc[:, lanes(head)] += nn_dot(p.astype(bf16), g)
            dk_acc[:, lanes(head)] += nn_dot(ds, q)

    def both_times(work, block):
        def body(index, carry):
            work(2 * index, block)
            return carry

        lax.fori_loop(0, 2, body, 0)

    def forward_side(dt, block):
        await_pair((KEY, VALUE), dt, block)
        forward_pair(3 * dt + block)

    def backward_side(dt, block):
        await_pair((QUERY, GRAD), dt, block)
        await_stats(dt, block)
        backward_pair(3 * dt + block)

    near, far = 2 * h, 2 - 2 * h

    for array in (KEY, VALUE):
        loads[array].wait()
        send_own(array)
        send_t(array, 2 + h)
    loads[QUERY].wait()
    send_t(QUERY, 2 + h)
    for load in loads[GRAD:]:
        load.wait()

    def zero_slot(index, carry):
        time_at, z_at = t + lax.div(index, 6) - 1, base + lax.rem(index, 6)

        @pl.when(jnp.logical_not(in_t(time_at) & in_z(z_at)))
        def _():
            for array in range(4):
                slots[array, index] = jnp.zeros((tokens, heads * head_dim), bf16)
            stats[index] = jnp.zeros((8, 256), f32)

        return carry

    lax.fori_loop(0, 18, zero_slot, 0)

    lane = lax.broadcasted_iota(jnp.int32, (1, pair), 1)
    for head in range(heads):
        reach_t, reach_h, reach_w = (window_ref[head, axis] for axis in range(3))
        for dt in range(3):
            for block in range(3):
                inside = (
                    in_t(t + dt - 1)
                    & (w + block - 1 >= 0)
                    & (w + block - 1 < n_cols)
                    & (abs(dt - 1) <= reach_t)
                    & (abs(block - 1) <= reach_w)
                )
                open_low = inside & (h <= reach_h)
                open_high = inside & (1 - h <= reach_h)
                low = jnp.where(open_low, 0.0, MASKED).astype(f32)
                high = jnp.where(open_high, 0.0, MASKED).astype(f32)
                bias[head * 9 + dt * 3 + block] = jnp.where(lane < tokens, low, high)

    for head in range(heads):
        q = slots[QUERY, mine, :, lanes(head)]
        g = slots[GRAD, mine, :, lanes(head)]
        s = nt_dot(q, text[0, :, lanes(head)])
        text_scores[head] = s
        top = s[:, :128]
        for at in range(128, n_text, 128):
            top = jnp.maximum(top, s[:, at : at + 128])
        peak[head] = top
        text_probs[head] = nt_dot(g, text[1, :, lanes(head)])
    dk_acc[...] = jnp.zeros_like(dk_acc)
    dv_acc[...] = jnp.zeros_like(dv_acc)

    arrive(KEY, 1)
    arrive(VALUE, 1)
    forward_pair(4)
    arrive(KEY, 2)
    both_times(forward_side, 1)
    arrive(VALUE, 2)
    send_own(QUERY)
    send_own(GRAD)
    forward_pair(3 + near)
    arrive(KEY, 3)
    send_t(GRAD, 2 + h)
    both_times(forward_side, near)
    arrive(QUERY, 1, (0,))
    arrive(VALUE, 3)
    forward_pair(3 + far)
    arrive(GRAD, 1, (0,))
    both_times(forward_side, far)
    arrive(QUERY, 1, (1,))

    row_lane = lax.broadcasted_iota(jnp.int32, (tokens, 128), 1)
    columns = jnp.zeros((tokens, 128), f32)
    inverse, dots = [], []
    for head in range(heads):
        if head == heads - 1:
            arrive(GRAD, 1, (1,))
        top = jnp.max(peak[head], axis=1, keepdims=True) * factor
        p = jnp.exp2(text_scores[head] * factor - top)
        total = p[:, :128]
        for at in range(128, n_text, 128):
            total = total + p[:, at : at + 128]
        p = p.astype(bf16)
        text_weights[head] = p
        acc = nn_dot(p, text[1, :, lanes(head)])

        def weigh(j, carry, head=head, top=top):
            total, acc = carry
            p = jnp.exp2(scores[head * 9 + j] * factor - top)
            for at in range(0, pair, 128):
                total = total + p[:, at : at + 128]
            p = p.astype(bf16)
            weights[head * 9 + j] = p
            return total, acc + nn_dot(p, pair_of(VALUE, j, head))

        total, acc = lax.fori_loop(0, 9, weigh, (total, acc))
        total = jnp.sum(total, axis=1, keepdims=True)
        inv = 1.0 / total
        out = (acc * inv).astype(bf16)
        out_ref[:, lanes(head)] = out
        g = slots[GRAD, mine, :, lanes(head)].astype(f32)
        dot = jnp.sum(g * out.astype(f32), axis=1, keepdims=True)
        inverse.append(inv)
        dots.append(dot)
        columns = jnp.where(row_lane == head, top + jnp.log2(total), columns)
        columns = jnp.where(row_lane == heads + head, dot, columns)

    own_stats = jnp.transpose(columns)[:8]
    stats[mine, :, :tokens] = own_stats
    send_stats()

    for head in range(heads):
        q = slots[QUERY, mine, :, lanes(head)]
        g = slots[GRAD, mine, :, lanes(head)]
        p = jnp.exp2(nt_dot(text[0, :, lanes(head)], q) * factor - own_stats[head : head + 1])
        d = nt_dot(text[1, :, lanes(head)], g)
        ds = (p * (d - own_stats[heads + head : heads + head + 1])).astype(bf16)
        dtv = nn_dot(p.astype(bf16), g).astype(bf16)
        dtk = (nn_dot(ds, q) * scale).astype(bf16)
        for part in range(n_time):
            rows = slice(part * rows_time, (part + 1) * rows_time)
            text_send[part % 2, part // 2, 0, :, lanes(head)] = dtk[rows]
            text_send[part % 2, part // 2, 1, :, lanes(head)] = dtv[rows]

    core, chip = lax.rem(t, 2), lax.div(t, 2)
    n_chips = n_time // 2
    core_copy = pltpu.make_async_remote_copy(
        src_ref=text_send.at[1 - core],
        dst_ref=text_near,
        send_sem=part_send.at[0],
        recv_sem=core_recv,
        device_id={"ta": t + 1 - 2 * core},
        device_id_type=MESH,
    )
    core_copy.start()
    arrive(QUERY, 2)

    def part_copy(step):
        there = lax.rem(chip + step, n_chips)
        return pltpu.make_async_remote_copy(
            src_ref=text_far.at[there],
            dst_ref=text_recv.at[chip],
            send_sem=part_send.at[step],
            recv_sem=part_recv.at[chip],
            device_id={"ta": 2 * there + core},
            device_id_type=MESH,
        )

    def sum_cores():
        core_copy.wait()
        for part in range(n_chips):
            text_far[part] = (text_send[core, part].astype(f32) + text_near[part].astype(f32)).astype(bf16)
        for step in range(1, n_chips):
            part_copy(step).start()
        text_recv[chip] = text_far[chip]

    for head in range(heads):
        dot = dots[head]
        ds = (text_weights[head].astype(f32) * (text_probs[head] - dot)).astype(bf16)
        acc = nn_dot(ds, text[0, :, lanes(head)])

        def pull(j, acc, head=head, dot=dot):
            ds = (weights[head * 9 + j].astype(f32) * (probs[head * 9 + j] - dot)).astype(bf16)
            return acc + nn_dot(ds, pair_of(KEY, j, head))

        acc = lax.fori_loop(0, 9, pull, acc)
        dq_ref[:, lanes(head)] = (acc * (inverse[head] * scale)).astype(bf16)
        if head == 0:
            sum_cores()
            arrive(GRAD, 2, (0,))
    arrive(GRAD, 2, (1,))
    arrive_stats()

    backward_pair(4)

    for step in range(1, n_chips):
        src = lax.rem(chip + step, n_chips)
        pltpu.make_async_copy(text_recv.at[src], text_recv.at[src], part_recv.at[src]).wait()
    summed = text_recv[0].astype(f32)
    for src in range(1, n_chips):
        summed = summed + text_recv[src].astype(f32)
    for part in range(n_z):
        rows = slice(part * rows_dev, (part + 1) * rows_dev)
        sum_send[part, 0:rows_dev] = summed[0, rows]
        sum_send[part, rows_dev : 2 * rows_dev] = summed[1, rows]

    def total_copy(step):
        there = lax.rem(z + step, n_z)
        to_h, to_w = lax.rem(there, n_rows), lax.div(there, n_rows)
        return pltpu.make_async_remote_copy(
            src_ref=sum_send.at[to_h * n_cols + to_w],
            dst_ref=sum_recv.at[z],
            send_sem=total_send.at[step],
            recv_sem=total_recv.at[z],
            device_id=z_device(there),
            device_id_type=MESH,
        )

    for step in range(1, n_z):
        total_copy(step).start()
    sum_recv[z] = sum_send[h * n_cols + w]

    backward_pair(3 + near)
    arrive(QUERY, 3)
    both_times(backward_side, 1)

    settle(KEY)
    settle(VALUE)
    arrive(GRAD, 3)
    both_times(backward_side, near)
    backward_pair(3 + far)
    both_times(backward_side, far)

    dk_ref[...] = (dk_acc[...] * scale).astype(bf16)
    dv_ref[...] = dv_acc[...].astype(bf16)

    for step in range(1, n_z):
        src = lax.rem(z + step, n_z)
        pltpu.make_async_copy(sum_recv.at[src], sum_recv.at[src], total_recv.at[src]).wait()
    final = sum_recv[0]
    for src in range(1, n_z):
        final = final + sum_recv[src]
    dtk_ref[...] = final[0:rows_dev].astype(bf16)
    dtv_ref[...] = final[rows_dev : 2 * rows_dev].astype(bf16)

    settle(QUERY)
    settle(GRAD)
    for spot in range(6):
        @pl.when(stat_wanted(spot))
        def _():
            stat_copy(spot).wait_send()

        for way in (1, -1):
            @pl.when(in_t(t + way) & in_z(base + spot))
            def _():
                stat_side_copy(spot, way).wait_send()

    for step in range(1, n_chips):
        part_copy(step).wait_send()
    for step in range(1, n_z):
        total_copy(step).wait_send()


def finish(*refs):
    moves = [pltpu.make_async_copy(refs[at], refs[6 + at], refs[12].at[at]) for at in range(6)]
    for move in moves:
        move.start()
    for move in moves:
        move.wait()


def on_device(query, keys, values, grad_out, text_keys, text_values, window):
    bf16, f32 = jnp.bfloat16, jnp.float32
    frames, height, wide, chans = query.shape
    heads = window.shape[0]
    head_dim = chans // heads
    tokens = frames * height * wide
    n_text = text_keys.shape[0]
    n_time, n_rows, n_cols = (lax.axis_size(axis) for axis in ("ta", "ha", "wa"))
    n_z = n_rows * n_cols
    rows_time = n_text // n_time
    rows_dev = rows_time // n_z
    sizes = (n_time, n_rows, n_cols, heads, head_dim, tokens, n_text)
    pair = 2 * tokens
    tile = jax.ShapeDtypeStruct((tokens, chans), bf16)
    text = jax.ShapeDtypeStruct((rows_dev, chans), bf16)
    held = [pltpu.VMEM(leaf.shape, bf16) for leaf in (tile, tile, tile, tile, text, text)]
    anywhere = pl.BlockSpec(memory_space=pl.ANY)
    vmem = pl.BlockSpec(memory_space=pltpu.VMEM)
    smem = pl.BlockSpec(memory_space=pltpu.SMEM)
    dma = pltpu.SemaphoreType.DMA
    flat = [array.reshape(tokens, chans) for array in (keys, values, query, grad_out)]
    results = pl.pallas_call(
        functools.partial(kernel, sizes),
        out_shape=held,
        in_specs=[anywhere] * 6 + [smem],
        out_specs=(vmem,) * 6,
        scratch_shapes=[
            pltpu.VMEM((4, 18, tokens, chans), bf16),
            pltpu.VMEM((2, n_text, chans), bf16),
            pltpu.VMEM((9 * heads, tokens, pair), f32),
            pltpu.VMEM((heads, tokens, n_text), f32),
            pltpu.VMEM((9 * heads, tokens, pair), f32),
            pltpu.VMEM((heads, tokens, n_text), f32),
            pltpu.VMEM((9 * heads, tokens, pair), bf16),
            pltpu.VMEM((heads, tokens, n_text), bf16),
            pltpu.VMEM((9 * heads, 1, pair), f32),
            pltpu.VMEM((heads, tokens, 128), f32),
            pltpu.VMEM((18, 8, 256), f32),
            pltpu.VMEM((tokens, chans), f32),
            pltpu.VMEM((tokens, chans), f32),
            pltpu.VMEM((2, n_time // 2, 2, rows_time, chans), bf16),
            pltpu.VMEM((n_time // 2, 2, rows_time, chans), bf16),
            pltpu.VMEM((n_time // 2, 2, rows_time, chans), bf16),
            pltpu.VMEM((n_time // 2, 2, rows_time, chans), bf16),
            pltpu.VMEM((n_z, 2 * rows_dev, chans), f32),
            pltpu.VMEM((n_z, 2 * rows_dev, chans), f32),
            dma((6,)),
            dma((4, 3)),
            dma((4, 3)),
            dma((4, 2, 6)),
            dma((4, 18)),
            dma((18,)),
            dma((18,)),
            dma,
            dma((n_time // 2,)),
            dma((n_time // 2,)),
            dma((n_z,)),
            dma((n_z,)),
        ],
        compiler_params=pltpu.CompilerParams(
            collective_id=0, has_side_effects=True, vmem_limit_bytes=56 * 1024 * 1024
        ),
    )(*flat, text_keys, text_values, window)
    out, dq, dk, dv, dtk, dtv = pl.pallas_call(
        finish,
        out_shape=(tile, tile, tile, tile, text, text),
        in_specs=[vmem] * 6,
        out_specs=(anywhere,) * 6,
        scratch_shapes=[dma((6,))],
    )(*[pltpu.with_memory_space_constraint(result, pltpu.VMEM) for result in results])
    shape = (frames, height, wide, chans)
    return tuple(array.reshape(shape) for array in (out, dq, dk, dv)) + (dtk, dtv)


def solution(mesh):
    tiled = P("ta", "ha", "wa", "head")
    placed = (tiled, tiled, tiled, tiled, P(None, "head"), P(None, "head"), P("head", None))
    text = P(("ta", "ha", "wa"), "head")
    return jax.shard_map(
        on_device,
        mesh=mesh,
        in_specs=placed,
        out_specs=(tiled, tiled, tiled, tiled, text, text),
        check_vma=False,
    )
```

```python
import functools

import jax
import jax.numpy as jnp
from jax import lax
from jax.experimental import pallas as pl
from jax.experimental.pallas import tpu as pltpu
from jax.sharding import PartitionSpec as P

MESH = pl.DeviceIdType.MESH
MASKED = -1e30
LOG2E = 1.4426950408889634
KEY, VALUE, QUERY, GRAD = 0, 1, 2, 3
PIECES = 1


def nt_dot(a, b):
    return lax.dot_general(a, b, (((1,), (1,)), ((), ())), preferred_element_type=jnp.float32)


def nn_dot(a, b):
    return jnp.dot(a, b, preferred_element_type=jnp.float32)


def kernel(
    sizes,
    keys_ref, values_ref, query_ref, grad_ref, text_key_in, text_value_in, window_in,
    out_ref, dq_ref, dk_ref, dv_ref, dtk_ref, dtv_ref,
    window_ref, slots, text, scores, text_scores, probs, text_probs, weights, text_weights,
    bias, peak, level, fade, stats, acc, totals, dk_acc, dv_acc,
    text_send, text_near, text_far, text_recv, sum_send, sum_recv,
    load_sem, up_send, down_send, side_send, slot_recv, stat_send, stat_recv,
    core_recv, part_send, part_recv, total_send, total_recv,
):
    n_time, n_rows, n_cols, heads, head_dim, tokens, n_text = sizes
    f32, bf16 = jnp.float32, jnp.bfloat16
    scale = head_dim ** -0.5
    factor = scale * LOG2E
    n_z = n_rows * n_cols
    rows_time = n_text // n_time
    rows_dev = rows_time // n_z
    pair = 2 * tokens

    t = lax.axis_index("ta")
    h = lax.axis_index("ha")
    w = lax.axis_index("wa")
    z = n_rows * w + h
    base = n_rows * (w - 1)
    mine = 6 + 2 + h

    def z_device(at):
        return {"ha": lax.rem(at, n_rows), "wa": lax.div(at, n_rows)}

    def in_z(at):
        return (at >= 0) & (at < n_z)

    def in_t(at):
        return (at >= 0) & (at < n_time)

    def lanes(head):
        return slice(head * head_dim, (head + 1) * head_dim)

    loads = [
        pltpu.make_async_copy(ref, slots.at[array, mine], load_sem.at[array])
        for array, ref in ((KEY, keys_ref), (VALUE, values_ref), (QUERY, query_ref), (GRAD, grad_ref))
    ]
    loads += [
        pltpu.make_async_copy(ref, text.at[at], load_sem.at[4 + at])
        for at, ref in enumerate((text_key_in, text_value_in))
    ]
    loads.append(pltpu.make_async_copy(window_in, window_ref, load_sem.at[6]))
    for load in loads:
        load.start()

    barrier = pltpu.get_barrier_semaphore()
    for step in range(1, n_time):
        pl.semaphore_signal(barrier, 1, device_id={"ta": lax.rem(t + step, n_time)}, device_id_type=MESH)
    for step in range(1, n_z):
        pl.semaphore_signal(barrier, 1, device_id=z_device(lax.rem(z + step, n_z)), device_id_type=MESH)
    pl.semaphore_wait(barrier, n_time - 1 + n_z - 1)

    def pieces(array):
        count = PIECES if array == GRAD else 1
        return [(at, pl.ds(at * (tokens // count), tokens // count)) for at in range(count)]

    def z_copy(array, step, way, piece):
        at, rows = piece
        tile = z - way * step
        there = z + way
        there_base = n_rows * (lax.div(there + n_rows, n_rows) - 2)
        sems = up_send if way == 1 else down_send
        dst = 6 + tile - there_base
        return pltpu.make_async_remote_copy(
            src_ref=slots.at[array, 6 + tile - base, rows],
            dst_ref=slots.at[array, dst, rows],
            send_sem=sems.at[array, step, at],
            recv_sem=slot_recv.at[array, dst, at],
            device_id=z_device(there),
            device_id_type=MESH,
        )

    def z_wanted(step, way):
        ok = in_z(z + way) & in_z(z - way * step)
        if step == 2:
            ok = ok & (h == (0 if way == 1 else 1))
        return ok

    def t_copy(array, spot, way, piece):
        at, rows = piece
        dst = 6 - 6 * way + spot
        return pltpu.make_async_remote_copy(
            src_ref=slots.at[array, 6 + spot, rows],
            dst_ref=slots.at[array, dst, rows],
            send_sem=side_send.at[array, (way + 1) // 2, spot, at],
            recv_sem=slot_recv.at[array, dst, at],
            device_id={"ta": t + way},
            device_id_type=MESH,
        )

    def wait_piece(array, slot, piece):
        at, rows = piece
        held = slots.at[array, slot, rows]
        pltpu.make_async_copy(held, held, slot_recv.at[array, slot, at]).wait()

    def wait_slot(array, slot):
        for piece in pieces(array):
            wait_piece(array, slot, piece)

    def send_z(array, step, way, piece):
        @pl.when(z_wanted(step, way))
        def _():
            z_copy(array, step, way, piece).start()

    def send_t(array, spot, piece):
        for way in (1, -1):
            @pl.when(in_t(t + way))
            def _():
                t_copy(array, spot, way, piece).start()

    def send_own(array):
        for piece in pieces(array):
            send_z(array, 0, 1, piece)
            send_z(array, 0, -1, piece)

    def send_own_side(array):
        for piece in pieces(array):
            send_t(array, 2 + h, piece)

    def settle(array):
        for way in (1, -1):
            for step in range(3):
                @pl.when(z_wanted(step, way))
                def _():
                    for piece in pieces(array):
                        z_copy(array, step, way, piece).wait_send()

            for spot in range(6):
                @pl.when(in_t(t + way) & in_z(base + spot))
                def _():
                    for piece in pieces(array):
                        t_copy(array, spot, way, piece).wait_send()

    def arrive(array, step, sides=(0, 1)):
        for side in sides if step < 3 else (1,):
            for way in (1, -1):
                tile = z - way * step
                ok = in_z(tile) & (h == (side if way == 1 else 1 - side))

                @pl.when(ok)
                def _():
                    for piece in pieces(array):
                        wait_piece(array, 6 + tile - base, piece)
                        if step < 3:
                            send_z(array, step, way, piece)
                        send_t(array, tile - base, piece)

    def await_pair(arrays, dt, block):
        for spot in (2 * block, 2 * block + 1):
            @pl.when(in_t(t + dt - 1) & in_z(base + spot))
            def _():
                for array in arrays:
                    wait_slot(array, 6 * dt + spot)

    def stat_copy(spot):
        dst = 6 + h + 4 - 2 * (spot // 2)
        return pltpu.make_async_remote_copy(
            src_ref=stats.at[mine],
            dst_ref=stats.at[dst],
            send_sem=stat_send.at[6 + spot],
            recv_sem=stat_recv.at[dst],
            device_id=z_device(base + spot),
            device_id_type=MESH,
        )

    def stat_wanted(spot):
        ok = in_z(base + spot)
        return ok & (spot != 2 + h) if spot in (2, 3) else ok

    def stat_side_copy(spot, way):
        dst = 6 - 6 * way + spot
        return pltpu.make_async_remote_copy(
            src_ref=stats.at[6 + spot],
            dst_ref=stats.at[dst],
            send_sem=stat_send.at[6 + 6 * way + spot],
            recv_sem=stat_recv.at[dst],
            device_id={"ta": t + way},
            device_id_type=MESH,
        )

    def wait_stat(slot):
        pltpu.make_async_copy(stats.at[slot], stats.at[slot], stat_recv.at[slot]).wait()

    def pass_stats(spot):
        for way in (1, -1):
            @pl.when(in_t(t + way))
            def _():
                stat_side_copy(spot, way).start()

    def send_stats():
        for spot in range(6):
            @pl.when(stat_wanted(spot))
            def _():
                stat_copy(spot).start()
        pass_stats(2 + h)

    def arrive_stats():
        for spot in range(6):
            @pl.when(stat_wanted(spot))
            def _():
                wait_stat(6 + spot)
                pass_stats(spot)

    def await_stats(dt, block):
        for spot in (2 * block, 2 * block + 1):
            @pl.when(in_t(t + dt - 1) & in_z(base + spot))
            def _():
                wait_stat(6 * dt + spot)

    def pair_of(array, j, head):
        return slots[array, pl.ds(2 * j, 2), :, lanes(head)].reshape(pair, head_dim)

    def forward_pair(j):
        for head in range(heads):
            q = slots[QUERY, mine, :, lanes(head)]
            g = slots[GRAD, mine, :, lanes(head)]
            s = nt_dot(q, pair_of(KEY, j, head)) + bias[head * 9 + j]
            scores[head * 9 + j] = s
            top = peak[head]
            for at in range(0, pair, 128):
                top = jnp.maximum(top, s[:, at : at + 128])
            peak[head] = top
            probs[head * 9 + j] = nt_dot(g, pair_of(VALUE, j, head))

    def backward(head, q, g, norm, dot):
        s = nt_dot(slots[KEY, mine, :, lanes(head)], q)
        p = jnp.exp2(s * factor - norm)
        d = nt_dot(slots[VALUE, mine, :, lanes(head)], g)
        ds = (p * (d - dot)).astype(bf16)
        dv_acc[:, lanes(head)] += nn_dot(p.astype(bf16), g)
        dk_acc[:, lanes(head)] += nn_dot(ds, q)

    def backward_pair(j):
        both = jnp.concatenate([stats[2 * j, :, :tokens], stats[2 * j + 1, :, :tokens]], axis=1)
        for head in range(heads):
            norm = both[head : head + 1] - bias[head * 9 + j]
            dot = both[heads + head : heads + head + 1]
            backward(head, pair_of(QUERY, j, head), pair_of(GRAD, j, head), norm, dot)

    def backward_far(dt, step):
        slot = 6 * dt + (4 - 3 * h if step == 2 else 5 - 5 * h)

        @pl.when(in_t(t + dt - 1) & in_z(base + slot - 6 * dt))
        def _():
            wait_slot(QUERY, slot)
            wait_slot(GRAD, slot)
            wait_stat(slot)

        upper = h == (1 if step == 2 else 0)
        for head in range(heads):
            row = bias[head * 9 + 3 * dt + far]
            masks = jnp.where(upper, row[:, tokens:], row[:, :tokens])
            norm = stats[slot, head : head + 1, :tokens] - masks
            dot = stats[slot, heads + head : heads + head + 1, :tokens]
            backward(head, slots[QUERY, slot, :, lanes(head)], slots[GRAD, slot, :, lanes(head)], norm, dot)

    def early_pair(index):
        return index + h + (index >= 2 + 3 * h).astype(jnp.int32)

    def weigh(j, carry):
        for head in range(heads):
            p = jnp.exp2(scores[head * 9 + j] * factor - level[head][:, :1])
            total = totals[:, lanes(head)]
            for at in range(0, pair, 128):
                total = total + p[:, at : at + 128]
            totals[:, lanes(head)] = total
            p = p.astype(bf16)
            weights[head * 9 + j] = p
            acc[:, lanes(head)] += nn_dot(p, pair_of(VALUE, j, head))
        return carry

    def begin_softmax():
        for head in range(heads):
            top = jnp.max(peak[head], axis=1, keepdims=True) * factor
            level[head] = jnp.broadcast_to(top, (tokens, 128))
            p = jnp.exp2(text_scores[head] * factor - top)
            total = p[:, :128]
            for at in range(128, n_text, 128):
                total = total + p[:, at : at + 128]
            p = p.astype(bf16)
            text_weights[head] = p
            totals[:, lanes(head)] = total
            acc[:, lanes(head)] = nn_dot(p, text[1, :, lanes(head)])
        lax.fori_loop(0, 7, lambda index, carry: weigh(early_pair(index), carry), 0)

    def both_times(work, block):
        def body(index, carry):
            work(2 * index, block)
            return carry

        lax.fori_loop(0, 2, body, 0)

    def forward_side(dt, block):
        await_pair((KEY, VALUE), dt, block)
        forward_pair(3 * dt + block)

    def backward_side(dt, block):
        await_pair((QUERY, GRAD), dt, block)
        await_stats(dt, block)
        backward_pair(3 * dt + block)

    near, far = 2 * h, 2 - 2 * h

    for array in (KEY, VALUE):
        loads[array].wait()
        send_own(array)
        send_own_side(array)
    loads[QUERY].wait()
    for load in loads[GRAD:]:
        load.wait()

    def zero_slot(index, carry):
        time_at, z_at = t + lax.div(index, 6) - 1, base + lax.rem(index, 6)

        @pl.when(jnp.logical_not(in_t(time_at) & in_z(z_at)))
        def _():
            for array in range(4):
                slots[array, index] = jnp.zeros((tokens, heads * head_dim), bf16)
            stats[index] = jnp.zeros((8, 256), f32)

        return carry

    lax.fori_loop(0, 18, zero_slot, 0)

    lane = lax.broadcasted_iota(jnp.int32, (1, pair), 1)
    for head in range(heads):
        reach_t, reach_h, reach_w = (window_ref[head, axis] for axis in range(3))
        for dt in range(3):
            for block in range(3):
                inside = (
                    in_t(t + dt - 1)
                    & (w + block - 1 >= 0)
                    & (w + block - 1 < n_cols)
                    & (abs(dt - 1) <= reach_t)
                    & (abs(block - 1) <= reach_w)
                )
                open_low = inside & (h <= reach_h)
                open_high = inside & (1 - h <= reach_h)
                low = jnp.where(open_low, 0.0, MASKED).astype(f32)
                high = jnp.where(open_high, 0.0, MASKED).astype(f32)
                bias[head * 9 + dt * 3 + block] = jnp.where(lane < tokens, low, high)

    for head in range(heads):
        q = slots[QUERY, mine, :, lanes(head)]
        g = slots[GRAD, mine, :, lanes(head)]
        s = nt_dot(q, text[0, :, lanes(head)])
        text_scores[head] = s
        top = s[:, :128]
        for at in range(128, n_text, 128):
            top = jnp.maximum(top, s[:, at : at + 128])
        peak[head] = top
        text_probs[head] = nt_dot(g, text[1, :, lanes(head)])
    dk_acc[...] = jnp.zeros_like(dk_acc)
    dv_acc[...] = jnp.zeros_like(dv_acc)

    arrive(KEY, 1)
    arrive(VALUE, 1)
    forward_pair(4)
    arrive(KEY, 2)
    both_times(forward_side, 1)
    arrive(VALUE, 2)
    send_own(QUERY)
    send_own(GRAD)
    forward_pair(3 + near)
    arrive(KEY, 3)
    both_times(forward_side, near)
    arrive(QUERY, 1, (0,))
    arrive(VALUE, 3)
    send_own_side(QUERY)
    send_own_side(GRAD)
    forward_pair(3 + far)
    begin_softmax()
    arrive(GRAD, 1, (0,))
    both_times(forward_side, far)
    arrive(QUERY, 1, (1,))
    arrive(GRAD, 1, (1,))

    for head in range(heads):
        early = level[head]
        top = jnp.max(peak[head], axis=1, keepdims=True) * factor
        level[head] = jnp.broadcast_to(top, (tokens, 128))
        fade[head] = jnp.exp2(early - level[head])
        totals[:, lanes(head)] *= fade[head]
        acc[:, lanes(head)] *= fade[head]
    weigh(far, 0)
    weigh(6 + far, 0)

    row_lane = lax.broadcasted_iota(jnp.int32, (tokens, 128), 1)
    columns = jnp.zeros((tokens, 128), f32)
    inverse, dots = [], []
    for head in range(heads):
        total = jnp.sum(totals[:, lanes(head)], axis=1, keepdims=True)
        inv = 1.0 / total
        out = (acc[:, lanes(head)] * inv).astype(bf16)
        out_ref[:, lanes(head)] = out
        g = slots[GRAD, mine, :, lanes(head)].astype(f32)
        dot = jnp.sum(g * out.astype(f32), axis=1, keepdims=True)
        inverse.append(inv)
        dots.append(dot)
        columns = jnp.where(row_lane == head, level[head] + jnp.log2(total), columns)
        columns = jnp.where(row_lane == heads + head, dot, columns)
        peak[head] = jnp.broadcast_to(dot, (tokens, 128))

    own_stats = jnp.transpose(columns)[:8]
    stats[mine, :, :tokens] = own_stats
    send_stats()

    for head in range(heads):
        q = slots[QUERY, mine, :, lanes(head)]
        g = slots[GRAD, mine, :, lanes(head)]
        p = jnp.exp2(nt_dot(text[0, :, lanes(head)], q) * factor - own_stats[head : head + 1])
        d = nt_dot(text[1, :, lanes(head)], g)
        ds = (p * (d - own_stats[heads + head : heads + head + 1])).astype(bf16)
        dtv = nn_dot(p.astype(bf16), g).astype(bf16)
        dtk = (nn_dot(ds, q) * scale).astype(bf16)
        for part in range(n_time):
            rows = slice(part * rows_time, (part + 1) * rows_time)
            text_send[part % 2, part // 2, 0, :, lanes(head)] = dtk[rows]
            text_send[part % 2, part // 2, 1, :, lanes(head)] = dtv[rows]

    core, chip = lax.rem(t, 2), lax.div(t, 2)
    n_chips = n_time // 2
    core_copy = pltpu.make_async_remote_copy(
        src_ref=text_send.at[1 - core],
        dst_ref=text_near,
        send_sem=part_send.at[0],
        recv_sem=core_recv,
        device_id={"ta": t + 1 - 2 * core},
        device_id_type=MESH,
    )
    core_copy.start()
    arrive(QUERY, 2)

    def part_copy(step):
        there = lax.rem(chip + step, n_chips)
        return pltpu.make_async_remote_copy(
            src_ref=text_far.at[there],
            dst_ref=text_recv.at[chip],
            send_sem=part_send.at[step],
            recv_sem=part_recv.at[chip],
            device_id={"ta": 2 * there + core},
            device_id_type=MESH,
        )

    def sum_cores():
        core_copy.wait()
        for part in range(n_chips):
            text_far[part] = (text_send[core, part].astype(f32) + text_near[part].astype(f32)).astype(bf16)
        for step in range(1, n_chips):
            part_copy(step).start()
        text_recv[chip] = text_far[chip]

    for head in range(heads):
        ds = (text_weights[head].astype(f32) * (text_probs[head] - dots[head])).astype(bf16)
        acc[:, lanes(head)] = nn_dot(ds, text[0, :, lanes(head)])

    def pull(j, carry):
        for head in range(heads):
            dot = peak[head][:, :1]
            ds = (weights[head * 9 + j].astype(f32) * (probs[head * 9 + j] - dot)).astype(bf16)
            acc[:, lanes(head)] += nn_dot(ds, pair_of(KEY, j, head))
        return carry

    lax.fori_loop(0, 3, lambda index, carry: pull(early_pair(index), carry), 0)
    sum_cores()
    arrive(GRAD, 2, (0,))
    lax.fori_loop(3, 7, lambda index, carry: pull(early_pair(index), carry), 0)
    for head in range(heads):
        acc[:, lanes(head)] *= fade[head]
    pull(far, 0)
    pull(6 + far, 0)
    for head in range(heads):
        dq_ref[:, lanes(head)] = (acc[:, lanes(head)] * (inverse[head] * scale)).astype(bf16)
    arrive(GRAD, 2, (1,))
    arrive_stats()

    backward_pair(4)

    for step in range(1, n_chips):
        src = lax.rem(chip + step, n_chips)
        pltpu.make_async_copy(text_recv.at[src], text_recv.at[src], part_recv.at[src]).wait()
    summed = text_recv[0].astype(f32)
    for src in range(1, n_chips):
        summed = summed + text_recv[src].astype(f32)
    for part in range(n_z):
        rows = slice(part * rows_dev, (part + 1) * rows_dev)
        sum_send[part, 0:rows_dev] = summed[0, rows]
        sum_send[part, rows_dev : 2 * rows_dev] = summed[1, rows]

    def total_copy(step):
        there = lax.rem(z + step, n_z)
        to_h, to_w = lax.rem(there, n_rows), lax.div(there, n_rows)
        return pltpu.make_async_remote_copy(
            src_ref=sum_send.at[to_h * n_cols + to_w],
            dst_ref=sum_recv.at[z],
            send_sem=total_send.at[step],
            recv_sem=total_recv.at[z],
            device_id=z_device(there),
            device_id_type=MESH,
        )

    for step in range(1, n_z):
        total_copy(step).start()
    sum_recv[z] = sum_send[h * n_cols + w]

    backward_pair(3 + near)
    arrive(QUERY, 3)
    both_times(backward_side, 1)
    settle(KEY)
    settle(VALUE)
    arrive(GRAD, 3)
    both_times(backward_side, near)
    for dt in (0, 2):
        backward_far(dt, 2)
    backward_pair(3 + far)
    for dt in (0, 2):
        backward_far(dt, 3)

    dk_ref[...] = (dk_acc[...] * scale).astype(bf16)
    dv_ref[...] = dv_acc[...].astype(bf16)

    for step in range(1, n_z):
        src = lax.rem(z + step, n_z)
        pltpu.make_async_copy(sum_recv.at[src], sum_recv.at[src], total_recv.at[src]).wait()
    final = sum_recv[0]
    for src in range(1, n_z):
        final = final + sum_recv[src]
    dtk_ref[...] = final[0:rows_dev].astype(bf16)
    dtv_ref[...] = final[rows_dev : 2 * rows_dev].astype(bf16)

    settle(QUERY)
    settle(GRAD)
    for spot in range(6):
        @pl.when(stat_wanted(spot))
        def _():
            stat_copy(spot).wait_send()

        for way in (1, -1):
            @pl.when(in_t(t + way) & in_z(base + spot))
            def _():
                stat_side_copy(spot, way).wait_send()

    for step in range(1, n_chips):
        part_copy(step).wait_send()
    for step in range(1, n_z):
        total_copy(step).wait_send()


def finish(*refs):
    moves = [pltpu.make_async_copy(refs[at], refs[6 + at], refs[12].at[at]) for at in range(6)]
    for move in moves:
        move.start()
    for move in moves:
        move.wait()


def on_device(query, keys, values, grad_out, text_keys, text_values, window):
    bf16, f32 = jnp.bfloat16, jnp.float32
    frames, height, wide, chans = query.shape
    heads = window.shape[0]
    head_dim = chans // heads
    tokens = frames * height * wide
    n_text = text_keys.shape[0]
    n_time, n_rows, n_cols = (lax.axis_size(axis) for axis in ("ta", "ha", "wa"))
    n_z = n_rows * n_cols
    rows_time = n_text // n_time
    rows_dev = rows_time // n_z
    sizes = (n_time, n_rows, n_cols, heads, head_dim, tokens, n_text)
    pair = 2 * tokens
    tile = jax.ShapeDtypeStruct((tokens, chans), bf16)
    text = jax.ShapeDtypeStruct((rows_dev, chans), bf16)
    held = [pltpu.VMEM(leaf.shape, bf16) for leaf in (tile, tile, tile, tile, text, text)]
    anywhere = pl.BlockSpec(memory_space=pl.ANY)
    vmem = pl.BlockSpec(memory_space=pltpu.VMEM)
    dma = pltpu.SemaphoreType.DMA
    flat = [array.reshape(tokens, chans) for array in (keys, values, query, grad_out)]
    results = pl.pallas_call(
        functools.partial(kernel, sizes),
        out_shape=held,
        in_specs=[anywhere] * 7,
        out_specs=(vmem,) * 6,
        scratch_shapes=[
            pltpu.SMEM(window.shape, jnp.int32),
            pltpu.VMEM((4, 18, tokens, chans), bf16),
            pltpu.VMEM((2, n_text, chans), bf16),
            pltpu.VMEM((9 * heads, tokens, pair), f32),
            pltpu.VMEM((heads, tokens, n_text), f32),
            pltpu.VMEM((9 * heads, tokens, pair), f32),
            pltpu.VMEM((heads, tokens, n_text), f32),
            pltpu.VMEM((9 * heads, tokens, pair), bf16),
            pltpu.VMEM((heads, tokens, n_text), bf16),
            pltpu.VMEM((9 * heads, 1, pair), f32),
            pltpu.VMEM((heads, tokens, 128), f32),
            pltpu.VMEM((heads, tokens, 128), f32),
            pltpu.VMEM((heads, tokens, 128), f32),
            pltpu.VMEM((18, 8, 256), f32),
            pltpu.VMEM((tokens, chans), f32),
            pltpu.VMEM((tokens, chans), f32),
            pltpu.VMEM((tokens, chans), f32),
            pltpu.VMEM((tokens, chans), f32),
            pltpu.VMEM((2, n_time // 2, 2, rows_time, chans), bf16),
            pltpu.VMEM((n_time // 2, 2, rows_time, chans), bf16),
            pltpu.VMEM((n_time // 2, 2, rows_time, chans), bf16),
            pltpu.VMEM((n_time // 2, 2, rows_time, chans), bf16),
            pltpu.VMEM((n_z, 2 * rows_dev, chans), f32),
            pltpu.VMEM((n_z, 2 * rows_dev, chans), f32),
            dma((7,)),
            dma((4, 3, PIECES)),
            dma((4, 3, PIECES)),
            dma((4, 2, 6, PIECES)),
            dma((4, 18, PIECES)),
            dma((18,)),
            dma((18,)),
            dma,
            dma((n_time // 2,)),
            dma((n_time // 2,)),
            dma((n_z,)),
            dma((n_z,)),
        ],
        compiler_params=pltpu.CompilerParams(
            collective_id=0, has_side_effects=True, vmem_limit_bytes=56 * 1024 * 1024
        ),
    )(*flat, text_keys, text_values, window)
    out, dq, dk, dv, dtk, dtv = pl.pallas_call(
        finish,
        out_shape=(tile, tile, tile, tile, text, text),
        in_specs=[vmem] * 6,
        out_specs=(anywhere,) * 6,
        scratch_shapes=[dma((6,))],
    )(*[pltpu.with_memory_space_constraint(result, pltpu.VMEM) for result in results])
    shape = (frames, height, wide, chans)
    return tuple(array.reshape(shape) for array in (out, dq, dk, dv)) + (dtk, dtv)


def solution(mesh):
    tiled = P("ta", "ha", "wa", "head")
    placed = (tiled, tiled, tiled, tiled, P(None, "head"), P(None, "head"), P("head", None))
    text = P(("ta", "ha", "wa"), "head")
    return jax.shard_map(
        on_device,
        mesh=mesh,
        in_specs=placed,
        out_specs=(tiled, tiled, tiled, tiled, text, text),
        check_vma=False,
    )
```

```python
import functools

import jax
import jax.numpy as jnp
from jax import lax
from jax.experimental import pallas as pl
from jax.experimental.pallas import tpu as pltpu
from jax.sharding import PartitionSpec as P

MESH = pl.DeviceIdType.MESH
MASKED = -1e30
LOG2E = 1.4426950408889634
KEY, VALUE, QUERY, GRAD = 0, 1, 2, 3
PIECES = 1


def nt_dot(a, b):
    return lax.dot_general(a, b, (((1,), (1,)), ((), ())), preferred_element_type=jnp.float32)


def nn_dot(a, b):
    return jnp.dot(a, b, preferred_element_type=jnp.float32)


def kernel(
    sizes,
    keys_ref, values_ref, query_ref, grad_ref, text_key_in, text_value_in, window_in,
    out_ref, dq_ref, dk_ref, dv_ref, dtk_ref, dtv_ref,
    window_ref, slots, text, scores, text_scores, probs, text_probs, weights, text_weights,
    bias, peak, level, fade, stats, acc, totals, dk_acc, dv_acc,
    text_send, text_near, text_far, text_recv, sum_send, sum_recv,
    load_sem, up_send, down_send, side_send, slot_recv, stat_send, stat_recv,
    core_recv, part_send, part_recv, total_send, total_recv,
):
    n_time, n_rows, n_cols, heads, head_dim, tokens, n_text = sizes
    f32, bf16 = jnp.float32, jnp.bfloat16
    scale = head_dim ** -0.5
    factor = scale * LOG2E
    n_z = n_rows * n_cols
    rows_time = n_text // n_time
    rows_dev = rows_time // n_z
    pair = 2 * tokens

    t = lax.axis_index("ta")
    h = lax.axis_index("ha")
    w = lax.axis_index("wa")
    z = n_rows * w + h
    base = n_rows * (w - 1)
    mine = 6 + 2 + h

    def z_device(at):
        return {"ha": lax.rem(at, n_rows), "wa": lax.div(at, n_rows)}

    def in_z(at):
        return (at >= 0) & (at < n_z)

    def in_t(at):
        return (at >= 0) & (at < n_time)

    def lanes(head):
        return slice(head * head_dim, (head + 1) * head_dim)

    loads = [
        pltpu.make_async_copy(ref, slots.at[array, mine], load_sem.at[array])
        for array, ref in ((KEY, keys_ref), (VALUE, values_ref), (QUERY, query_ref), (GRAD, grad_ref))
    ]
    loads += [
        pltpu.make_async_copy(ref, text.at[at], load_sem.at[4 + at])
        for at, ref in enumerate((text_key_in, text_value_in))
    ]
    loads.append(pltpu.make_async_copy(window_in, window_ref, load_sem.at[6]))
    for load in loads:
        load.start()

    barrier = pltpu.get_barrier_semaphore()
    for step in range(1, n_time):
        pl.semaphore_signal(barrier, 1, device_id={"ta": lax.rem(t + step, n_time)}, device_id_type=MESH)
    for step in range(1, n_z):
        pl.semaphore_signal(barrier, 1, device_id=z_device(lax.rem(z + step, n_z)), device_id_type=MESH)
    pl.semaphore_wait(barrier, n_time - 1 + n_z - 1)

    def pieces(array):
        count = PIECES if array == GRAD else 1
        return [(at, pl.ds(at * (tokens // count), tokens // count)) for at in range(count)]

    def z_copy(array, step, way, piece):
        at, rows = piece
        tile = z - way * step
        there = z + way
        there_base = n_rows * (lax.div(there + n_rows, n_rows) - 2)
        sems = up_send if way == 1 else down_send
        dst = 6 + tile - there_base
        return pltpu.make_async_remote_copy(
            src_ref=slots.at[array, 6 + tile - base, rows],
            dst_ref=slots.at[array, dst, rows],
            send_sem=sems.at[array, step, at],
            recv_sem=slot_recv.at[array, dst, at],
            device_id=z_device(there),
            device_id_type=MESH,
        )

    def z_wanted(step, way):
        ok = in_z(z + way) & in_z(z - way * step)
        if step == 2:
            ok = ok & (h == (0 if way == 1 else 1))
        return ok

    def t_copy(array, spot, way, piece):
        at, rows = piece
        dst = 6 - 6 * way + spot
        return pltpu.make_async_remote_copy(
            src_ref=slots.at[array, 6 + spot, rows],
            dst_ref=slots.at[array, dst, rows],
            send_sem=side_send.at[array, (way + 1) // 2, spot, at],
            recv_sem=slot_recv.at[array, dst, at],
            device_id={"ta": t + way},
            device_id_type=MESH,
        )

    def wait_piece(array, slot, piece):
        at, rows = piece
        held = slots.at[array, slot, rows]
        pltpu.make_async_copy(held, held, slot_recv.at[array, slot, at]).wait()

    def wait_slot(array, slot):
        for piece in pieces(array):
            wait_piece(array, slot, piece)

    def send_z(array, step, way, piece):
        @pl.when(z_wanted(step, way))
        def _():
            z_copy(array, step, way, piece).start()

    def send_t(array, spot, piece):
        for way in (1, -1):
            @pl.when(in_t(t + way))
            def _():
                t_copy(array, spot, way, piece).start()

    def send_own(array):
        for piece in pieces(array):
            send_z(array, 0, 1, piece)
            send_z(array, 0, -1, piece)

    def send_own_side(array):
        for piece in pieces(array):
            send_t(array, 2 + h, piece)

    def settle(array):
        for way in (1, -1):
            for step in range(3):
                @pl.when(z_wanted(step, way))
                def _():
                    for piece in pieces(array):
                        z_copy(array, step, way, piece).wait_send()

            for spot in range(6):
                @pl.when(in_t(t + way) & in_z(base + spot))
                def _():
                    for piece in pieces(array):
                        t_copy(array, spot, way, piece).wait_send()

    def arrive(array, step, sides=(0, 1)):
        for side in sides if step < 3 else (1,):
            for way in (1, -1):
                tile = z - way * step
                ok = in_z(tile) & (h == (side if way == 1 else 1 - side))

                @pl.when(ok)
                def _():
                    for piece in pieces(array):
                        wait_piece(array, 6 + tile - base, piece)
                        if step < 3:
                            send_z(array, step, way, piece)
                        send_t(array, tile - base, piece)

    def await_pair(arrays, dt, block):
        for spot in (2 * block, 2 * block + 1):
            @pl.when(in_t(t + dt - 1) & in_z(base + spot))
            def _():
                for array in arrays:
                    wait_slot(array, 6 * dt + spot)

    def stat_copy(spot):
        dst = 6 + h + 4 - 2 * (spot // 2)
        return pltpu.make_async_remote_copy(
            src_ref=stats.at[mine],
            dst_ref=stats.at[dst],
            send_sem=stat_send.at[6 + spot],
            recv_sem=stat_recv.at[dst],
            device_id=z_device(base + spot),
            device_id_type=MESH,
        )

    def stat_wanted(spot):
        ok = in_z(base + spot)
        return ok & (spot != 2 + h) if spot in (2, 3) else ok

    def stat_side_copy(spot, way):
        dst = 6 - 6 * way + spot
        return pltpu.make_async_remote_copy(
            src_ref=stats.at[6 + spot],
            dst_ref=stats.at[dst],
            send_sem=stat_send.at[6 + 6 * way + spot],
            recv_sem=stat_recv.at[dst],
            device_id={"ta": t + way},
            device_id_type=MESH,
        )

    def wait_stat(slot):
        pltpu.make_async_copy(stats.at[slot], stats.at[slot], stat_recv.at[slot]).wait()

    def pass_stats(spot):
        for way in (1, -1):
            @pl.when(in_t(t + way))
            def _():
                stat_side_copy(spot, way).start()

    def send_stats():
        for spot in range(6):
            @pl.when(stat_wanted(spot))
            def _():
                stat_copy(spot).start()
        pass_stats(2 + h)

    def arrive_stats():
        for spot in range(6):
            @pl.when(stat_wanted(spot))
            def _():
                wait_stat(6 + spot)
                pass_stats(spot)

    def await_stats(dt, block):
        for spot in (2 * block, 2 * block + 1):
            @pl.when(in_t(t + dt - 1) & in_z(base + spot))
            def _():
                wait_stat(6 * dt + spot)

    def pair_of(array, j, head):
        return slots[array, pl.ds(2 * j, 2), :, lanes(head)].reshape(pair, head_dim)

    def forward_pair(j):
        for head in range(heads):
            q = slots[QUERY, mine, :, lanes(head)]
            g = slots[GRAD, mine, :, lanes(head)]
            s = nt_dot(q, pair_of(KEY, j, head)) + bias[head * 9 + j]
            scores[head * 9 + j] = s
            top = peak[head]
            for at in range(0, pair, 128):
                top = jnp.maximum(top, s[:, at : at + 128])
            peak[head] = top
            probs[head * 9 + j] = nt_dot(g, pair_of(VALUE, j, head))

    def backward(head, q, g, norm, dot):
        s = nt_dot(slots[KEY, mine, :, lanes(head)], q)
        p = jnp.exp2(s * factor - norm)
        d = nt_dot(slots[VALUE, mine, :, lanes(head)], g)
        ds = (p * (d - dot)).astype(bf16)
        dv_acc[:, lanes(head)] += nn_dot(p.astype(bf16), g)
        dk_acc[:, lanes(head)] += nn_dot(ds, q)

    def backward_pair(j):
        both = jnp.concatenate([stats[2 * j, :, :tokens], stats[2 * j + 1, :, :tokens]], axis=1)
        for head in range(heads):
            norm = both[head : head + 1] - bias[head * 9 + j]
            dot = both[heads + head : heads + head + 1]
            backward(head, pair_of(QUERY, j, head), pair_of(GRAD, j, head), norm, dot)

    def backward_far(dt, step):
        slot = 6 * dt + (4 - 3 * h if step == 2 else 5 - 5 * h)

        @pl.when(in_t(t + dt - 1) & in_z(base + slot - 6 * dt))
        def _():
            wait_slot(QUERY, slot)
            wait_slot(GRAD, slot)
            wait_stat(slot)

        upper = h == (1 if step == 2 else 0)
        for head in range(heads):
            row = bias[head * 9 + 3 * dt + far]
            masks = jnp.where(upper, row[:, tokens:], row[:, :tokens])
            norm = stats[slot, head : head + 1, :tokens] - masks
            dot = stats[slot, heads + head : heads + head + 1, :tokens]
            backward(head, slots[QUERY, slot, :, lanes(head)], slots[GRAD, slot, :, lanes(head)], norm, dot)

    def early_pair(index):
        return index + h + (index >= 2 + 3 * h).astype(jnp.int32)

    def weigh(j, carry):
        for head in range(heads):
            p = jnp.exp2(scores[head * 9 + j] * factor - level[head][:, :1])
            total = totals[:, lanes(head)]
            for at in range(0, pair, 128):
                total = total + p[:, at : at + 128]
            totals[:, lanes(head)] = total
            p = p.astype(bf16)
            weights[head * 9 + j] = p
            acc[:, lanes(head)] += nn_dot(p, pair_of(VALUE, j, head))
        return carry

    def begin_softmax():
        for head in range(heads):
            top = jnp.max(peak[head], axis=1, keepdims=True) * factor
            level[head] = jnp.broadcast_to(top, (tokens, 128))
            p = jnp.exp2(text_scores[head] * factor - top)
            total = p[:, :128]
            for at in range(128, n_text, 128):
                total = total + p[:, at : at + 128]
            p = p.astype(bf16)
            text_weights[head] = p
            totals[:, lanes(head)] = total
            acc[:, lanes(head)] = nn_dot(p, text[1, :, lanes(head)])
        lax.fori_loop(0, 7, lambda index, carry: weigh(early_pair(index), carry), 0)

    def both_times(work, block):
        def body(index, carry):
            work(2 * index, block)
            return carry

        lax.fori_loop(0, 2, body, 0)

    def forward_side(dt, block):
        await_pair((KEY, VALUE), dt, block)
        forward_pair(3 * dt + block)

    def backward_side(dt, block):
        await_pair((QUERY, GRAD), dt, block)
        await_stats(dt, block)
        backward_pair(3 * dt + block)

    near, far = 2 * h, 2 - 2 * h

    for array in (KEY, VALUE):
        loads[array].wait()
        send_own(array)
        send_own_side(array)
    loads[QUERY].wait()
    send_own_side(QUERY)
    for load in loads[GRAD:]:
        load.wait()

    def zero_slot(index, carry):
        time_at, z_at = t + lax.div(index, 6) - 1, base + lax.rem(index, 6)

        @pl.when(jnp.logical_not(in_t(time_at) & in_z(z_at)))
        def _():
            for array in range(4):
                slots[array, index] = jnp.zeros((tokens, heads * head_dim), bf16)
            stats[index] = jnp.zeros((8, 256), f32)

        return carry

    lax.fori_loop(0, 18, zero_slot, 0)

    lane = lax.broadcasted_iota(jnp.int32, (1, pair), 1)
    for head in range(heads):
        reach_t, reach_h, reach_w = (window_ref[head, axis] for axis in range(3))
        for dt in range(3):
            for block in range(3):
                inside = (
                    in_t(t + dt - 1)
                    & (w + block - 1 >= 0)
                    & (w + block - 1 < n_cols)
                    & (abs(dt - 1) <= reach_t)
                    & (abs(block - 1) <= reach_w)
                )
                open_low = inside & (h <= reach_h)
                open_high = inside & (1 - h <= reach_h)
                low = jnp.where(open_low, 0.0, MASKED).astype(f32)
                high = jnp.where(open_high, 0.0, MASKED).astype(f32)
                bias[head * 9 + dt * 3 + block] = jnp.where(lane < tokens, low, high)

    for head in range(heads):
        q = slots[QUERY, mine, :, lanes(head)]
        g = slots[GRAD, mine, :, lanes(head)]
        s = nt_dot(q, text[0, :, lanes(head)])
        text_scores[head] = s
        top = s[:, :128]
        for at in range(128, n_text, 128):
            top = jnp.maximum(top, s[:, at : at + 128])
        peak[head] = top
        text_probs[head] = nt_dot(g, text[1, :, lanes(head)])
    dk_acc[...] = jnp.zeros_like(dk_acc)
    dv_acc[...] = jnp.zeros_like(dv_acc)

    arrive(KEY, 1)
    arrive(VALUE, 1)
    forward_pair(4)
    arrive(KEY, 2)
    arrive(VALUE, 2)
    send_own(QUERY)
    send_own(GRAD)
    both_times(forward_side, 1)
    forward_pair(3 + near)
    arrive(KEY, 3)
    both_times(forward_side, near)
    arrive(QUERY, 1, (0,))
    arrive(VALUE, 3)
    send_own_side(GRAD)
    forward_pair(3 + far)
    begin_softmax()
    arrive(GRAD, 1, (0,))
    both_times(forward_side, far)
    arrive(QUERY, 1, (1,))

    for head in range(heads):
        early = level[head]
        top = jnp.max(peak[head], axis=1, keepdims=True) * factor
        level[head] = jnp.broadcast_to(top, (tokens, 128))
        fade[head] = jnp.exp2(early - level[head])
        totals[:, lanes(head)] *= fade[head]
        acc[:, lanes(head)] *= fade[head]
    weigh(far, 0)
    weigh(6 + far, 0)

    row_lane = lax.broadcasted_iota(jnp.int32, (tokens, 128), 1)
    columns = jnp.zeros((tokens, 128), f32)
    inverse, dots = [], []
    for head in range(heads):
        total = jnp.sum(totals[:, lanes(head)], axis=1, keepdims=True)
        inv = 1.0 / total
        out = (acc[:, lanes(head)] * inv).astype(bf16)
        out_ref[:, lanes(head)] = out
        g = slots[GRAD, mine, :, lanes(head)].astype(f32)
        dot = jnp.sum(g * out.astype(f32), axis=1, keepdims=True)
        inverse.append(inv)
        dots.append(dot)
        columns = jnp.where(row_lane == head, level[head] + jnp.log2(total), columns)
        columns = jnp.where(row_lane == heads + head, dot, columns)
        peak[head] = jnp.broadcast_to(dot, (tokens, 128))

    own_stats = jnp.transpose(columns)[:8]
    stats[mine, :, :tokens] = own_stats
    send_stats()
    arrive(GRAD, 1, (1,))

    for head in range(heads):
        q = slots[QUERY, mine, :, lanes(head)]
        g = slots[GRAD, mine, :, lanes(head)]
        p = jnp.exp2(nt_dot(text[0, :, lanes(head)], q) * factor - own_stats[head : head + 1])
        d = nt_dot(text[1, :, lanes(head)], g)
        ds = (p * (d - own_stats[heads + head : heads + head + 1])).astype(bf16)
        dtv = nn_dot(p.astype(bf16), g).astype(bf16)
        dtk = (nn_dot(ds, q) * scale).astype(bf16)
        for part in range(n_time):
            rows = slice(part * rows_time, (part + 1) * rows_time)
            text_send[part % 2, part // 2, 0, :, lanes(head)] = dtk[rows]
            text_send[part % 2, part // 2, 1, :, lanes(head)] = dtv[rows]

    core, chip = lax.rem(t, 2), lax.div(t, 2)
    n_chips = n_time // 2
    core_copy = pltpu.make_async_remote_copy(
        src_ref=text_send.at[1 - core],
        dst_ref=text_near,
        send_sem=part_send.at[0],
        recv_sem=core_recv,
        device_id={"ta": t + 1 - 2 * core},
        device_id_type=MESH,
    )
    core_copy.start()

    def part_copy(step):
        there = lax.rem(chip + step, n_chips)
        return pltpu.make_async_remote_copy(
            src_ref=text_far.at[there],
            dst_ref=text_recv.at[chip],
            send_sem=part_send.at[step],
            recv_sem=part_recv.at[chip],
            device_id={"ta": 2 * there + core},
            device_id_type=MESH,
        )

    def sum_cores():
        core_copy.wait()
        for part in range(n_chips):
            text_far[part] = (text_send[core, part].astype(f32) + text_near[part].astype(f32)).astype(bf16)
        for step in range(1, n_chips):
            part_copy(step).start()
        text_recv[chip] = text_far[chip]

    for head in range(heads):
        ds = (text_weights[head].astype(f32) * (text_probs[head] - dots[head])).astype(bf16)
        acc[:, lanes(head)] = nn_dot(ds, text[0, :, lanes(head)])

    def pull(j, carry):
        for head in range(heads):
            dot = peak[head][:, :1]
            ds = (weights[head * 9 + j].astype(f32) * (probs[head * 9 + j] - dot)).astype(bf16)
            acc[:, lanes(head)] += nn_dot(ds, pair_of(KEY, j, head))
        return carry

    lax.fori_loop(0, 3, lambda index, carry: pull(early_pair(index), carry), 0)
    sum_cores()
    arrive(QUERY, 2)
    arrive(GRAD, 2, (0,))
    lax.fori_loop(3, 7, lambda index, carry: pull(early_pair(index), carry), 0)
    for head in range(heads):
        acc[:, lanes(head)] *= fade[head]
    pull(far, 0)
    pull(6 + far, 0)
    for head in range(heads):
        dq_ref[:, lanes(head)] = (acc[:, lanes(head)] * (inverse[head] * scale)).astype(bf16)
    arrive(GRAD, 2, (1,))
    arrive_stats()
    for step in range(1, n_chips):
        src = lax.rem(chip + step, n_chips)
        pltpu.make_async_copy(text_recv.at[src], text_recv.at[src], part_recv.at[src]).wait()
    summed = text_recv[0].astype(f32)
    for src in range(1, n_chips):
        summed = summed + text_recv[src].astype(f32)
    for part in range(n_z):
        rows = slice(part * rows_dev, (part + 1) * rows_dev)
        sum_send[part, 0:rows_dev] = summed[0, rows]
        sum_send[part, rows_dev : 2 * rows_dev] = summed[1, rows]

    def total_copy(step):
        there = lax.rem(z + step, n_z)
        to_h, to_w = lax.rem(there, n_rows), lax.div(there, n_rows)
        return pltpu.make_async_remote_copy(
            src_ref=sum_send.at[to_h * n_cols + to_w],
            dst_ref=sum_recv.at[z],
            send_sem=total_send.at[step],
            recv_sem=total_recv.at[z],
            device_id=z_device(there),
            device_id_type=MESH,
        )

    for step in range(1, n_z):
        total_copy(step).start()
    sum_recv[z] = sum_send[h * n_cols + w]


    backward_pair(4)

    backward_pair(3 + near)
    arrive(QUERY, 3)
    both_times(backward_side, 1)
    settle(KEY)
    settle(VALUE)
    arrive(GRAD, 3)
    both_times(backward_side, near)
    for dt in (0, 2):
        backward_far(dt, 2)
    backward_pair(3 + far)
    for dt in (0, 2):
        backward_far(dt, 3)

    dk_ref[...] = (dk_acc[...] * scale).astype(bf16)
    dv_ref[...] = dv_acc[...].astype(bf16)

    for step in range(1, n_z):
        src = lax.rem(z + step, n_z)
        pltpu.make_async_copy(sum_recv.at[src], sum_recv.at[src], total_recv.at[src]).wait()
    final = sum_recv[0]
    for src in range(1, n_z):
        final = final + sum_recv[src]
    dtk_ref[...] = final[0:rows_dev].astype(bf16)
    dtv_ref[...] = final[rows_dev : 2 * rows_dev].astype(bf16)

    settle(QUERY)
    settle(GRAD)
    for spot in range(6):
        @pl.when(stat_wanted(spot))
        def _():
            stat_copy(spot).wait_send()

        for way in (1, -1):
            @pl.when(in_t(t + way) & in_z(base + spot))
            def _():
                stat_side_copy(spot, way).wait_send()

    for step in range(1, n_chips):
        part_copy(step).wait_send()
    for step in range(1, n_z):
        total_copy(step).wait_send()


def finish(*refs):
    moves = [pltpu.make_async_copy(refs[at], refs[6 + at], refs[12].at[at]) for at in range(6)]
    for move in moves:
        move.start()
    for move in moves:
        move.wait()


def on_device(query, keys, values, grad_out, text_keys, text_values, window):
    bf16, f32 = jnp.bfloat16, jnp.float32
    frames, height, wide, chans = query.shape
    heads = window.shape[0]
    head_dim = chans // heads
    tokens = frames * height * wide
    n_text = text_keys.shape[0]
    n_time, n_rows, n_cols = (lax.axis_size(axis) for axis in ("ta", "ha", "wa"))
    n_z = n_rows * n_cols
    rows_time = n_text // n_time
    rows_dev = rows_time // n_z
    sizes = (n_time, n_rows, n_cols, heads, head_dim, tokens, n_text)
    pair = 2 * tokens
    tile = jax.ShapeDtypeStruct((tokens, chans), bf16)
    text = jax.ShapeDtypeStruct((rows_dev, chans), bf16)
    held = [pltpu.VMEM(leaf.shape, bf16) for leaf in (tile, tile, tile, tile, text, text)]
    anywhere = pl.BlockSpec(memory_space=pl.ANY)
    vmem = pl.BlockSpec(memory_space=pltpu.VMEM)
    dma = pltpu.SemaphoreType.DMA
    flat = [array.reshape(tokens, chans) for array in (keys, values, query, grad_out)]
    results = pl.pallas_call(
        functools.partial(kernel, sizes),
        out_shape=held,
        in_specs=[anywhere] * 7,
        out_specs=(vmem,) * 6,
        scratch_shapes=[
            pltpu.SMEM(window.shape, jnp.int32),
            pltpu.VMEM((4, 18, tokens, chans), bf16),
            pltpu.VMEM((2, n_text, chans), bf16),
            pltpu.VMEM((9 * heads, tokens, pair), f32),
            pltpu.VMEM((heads, tokens, n_text), f32),
            pltpu.VMEM((9 * heads, tokens, pair), f32),
            pltpu.VMEM((heads, tokens, n_text), f32),
            pltpu.VMEM((9 * heads, tokens, pair), bf16),
            pltpu.VMEM((heads, tokens, n_text), bf16),
            pltpu.VMEM((9 * heads, 1, pair), f32),
            pltpu.VMEM((heads, tokens, 128), f32),
            pltpu.VMEM((heads, tokens, 128), f32),
            pltpu.VMEM((heads, tokens, 128), f32),
            pltpu.VMEM((18, 8, 256), f32),
            pltpu.VMEM((tokens, chans), f32),
            pltpu.VMEM((tokens, chans), f32),
            pltpu.VMEM((tokens, chans), f32),
            pltpu.VMEM((tokens, chans), f32),
            pltpu.VMEM((2, n_time // 2, 2, rows_time, chans), bf16),
            pltpu.VMEM((n_time // 2, 2, rows_time, chans), bf16),
            pltpu.VMEM((n_time // 2, 2, rows_time, chans), bf16),
            pltpu.VMEM((n_time // 2, 2, rows_time, chans), bf16),
            pltpu.VMEM((n_z, 2 * rows_dev, chans), f32),
            pltpu.VMEM((n_z, 2 * rows_dev, chans), f32),
            dma((7,)),
            dma((4, 3, PIECES)),
            dma((4, 3, PIECES)),
            dma((4, 2, 6, PIECES)),
            dma((4, 18, PIECES)),
            dma((18,)),
            dma((18,)),
            dma,
            dma((n_time // 2,)),
            dma((n_time // 2,)),
            dma((n_z,)),
            dma((n_z,)),
        ],
        compiler_params=pltpu.CompilerParams(
            collective_id=0, has_side_effects=True, vmem_limit_bytes=56 * 1024 * 1024
        ),
    )(*flat, text_keys, text_values, window)
    out, dq, dk, dv, dtk, dtv = pl.pallas_call(
        finish,
        out_shape=(tile, tile, tile, tile, text, text),
        in_specs=[vmem] * 6,
        out_specs=(anywhere,) * 6,
        scratch_shapes=[dma((6,))],
    )(*[pltpu.with_memory_space_constraint(result, pltpu.VMEM) for result in results])
    shape = (frames, height, wide, chans)
    return tuple(array.reshape(shape) for array in (out, dq, dk, dv)) + (dtk, dtv)


def solution(mesh):
    tiled = P("ta", "ha", "wa", "head")
    placed = (tiled, tiled, tiled, tiled, P(None, "head"), P(None, "head"), P("head", None))
    text = P(("ta", "ha", "wa"), "head")
    return jax.shard_map(
        on_device,
        mesh=mesh,
        in_specs=placed,
        out_specs=(tiled, tiled, tiled, tiled, text, text),
        check_vma=False,
    )
```

```python
import functools

import jax
import jax.numpy as jnp
from jax import lax
from jax.experimental import pallas as pl
from jax.experimental.pallas import tpu as pltpu
from jax.sharding import PartitionSpec as P

MESH = pl.DeviceIdType.MESH
MASKED = -1e30
LOG2E = 1.4426950408889634
KEY, VALUE, QUERY, GRAD = 0, 1, 2, 3
PIECES = 1


def nt_dot(a, b):
    return lax.dot_general(a, b, (((1,), (1,)), ((), ())), preferred_element_type=jnp.float32)


def nn_dot(a, b):
    return jnp.dot(a, b, preferred_element_type=jnp.float32)


def kernel(
    sizes,
    keys_ref, values_ref, query_ref, grad_ref, text_key_in, text_value_in, window_in,
    out_ref, dq_ref, dk_ref, dv_ref, dtk_ref, dtv_ref,
    window_ref, slots, text, scores, text_scores, probs, text_probs, weights, text_weights,
    bias, peak, level, fade, stats, acc, totals, dk_acc, dv_acc,
    text_send, text_near, text_far, text_recv, sum_send, sum_recv,
    load_sem, up_send, down_send, side_send, slot_recv, stat_send, stat_recv,
    core_recv, part_send, part_recv, total_send, total_recv,
):
    n_time, n_rows, n_cols, heads, head_dim, tokens, n_text = sizes
    f32, bf16 = jnp.float32, jnp.bfloat16
    scale = head_dim ** -0.5
    factor = scale * LOG2E
    n_z = n_rows * n_cols
    rows_time = n_text // n_time
    rows_dev = rows_time // n_z
    pair = 2 * tokens

    t = lax.axis_index("ta")
    h = lax.axis_index("ha")
    w = lax.axis_index("wa")
    z = n_rows * w + h
    base = n_rows * (w - 1)
    mine = 6 + 2 + h

    def z_device(at):
        return {"ha": lax.rem(at, n_rows), "wa": lax.div(at, n_rows)}

    def in_z(at):
        return (at >= 0) & (at < n_z)

    def in_t(at):
        return (at >= 0) & (at < n_time)

    def lanes(head):
        return slice(head * head_dim, (head + 1) * head_dim)

    loads = [
        pltpu.make_async_copy(ref, slots.at[array, mine], load_sem.at[array])
        for array, ref in ((KEY, keys_ref), (VALUE, values_ref), (QUERY, query_ref), (GRAD, grad_ref))
    ]
    loads += [
        pltpu.make_async_copy(ref, text.at[at], load_sem.at[4 + at])
        for at, ref in enumerate((text_key_in, text_value_in))
    ]
    loads.append(pltpu.make_async_copy(window_in, window_ref, load_sem.at[6]))
    for load in loads:
        load.start()

    barrier = pltpu.get_barrier_semaphore()
    near_times = sorted({1, n_time - 1, *range(2, n_time, 2)})
    for step in near_times:
        pl.semaphore_signal(barrier, 1, device_id={"ta": lax.rem(t + step, n_time)}, device_id_type=MESH)
    for step in range(1, n_z):
        pl.semaphore_signal(barrier, 1, device_id=z_device(lax.rem(z + step, n_z)), device_id_type=MESH)
    pl.semaphore_wait(barrier, len(near_times) + n_z - 1)

    def pieces(array):
        count = PIECES if array == GRAD else 1
        return [(at, pl.ds(at * (tokens // count), tokens // count)) for at in range(count)]

    def z_copy(array, step, way, piece):
        at, rows = piece
        tile = z - way * step
        there = z + way
        there_base = n_rows * (lax.div(there + n_rows, n_rows) - 2)
        sems = up_send if way == 1 else down_send
        dst = 6 + tile - there_base
        return pltpu.make_async_remote_copy(
            src_ref=slots.at[array, 6 + tile - base, rows],
            dst_ref=slots.at[array, dst, rows],
            send_sem=sems.at[array, step, at],
            recv_sem=slot_recv.at[array, dst, at],
            device_id=z_device(there),
            device_id_type=MESH,
        )

    def z_wanted(step, way):
        ok = in_z(z + way) & in_z(z - way * step)
        if step == 2:
            ok = ok & (h == (0 if way == 1 else 1))
        return ok

    def t_copy(array, spot, way, piece):
        at, rows = piece
        dst = 6 - 6 * way + spot
        return pltpu.make_async_remote_copy(
            src_ref=slots.at[array, 6 + spot, rows],
            dst_ref=slots.at[array, dst, rows],
            send_sem=side_send.at[array, (way + 1) // 2, spot, at],
            recv_sem=slot_recv.at[array, dst, at],
            device_id={"ta": t + way},
            device_id_type=MESH,
        )

    def wait_piece(array, slot, piece):
        at, rows = piece
        held = slots.at[array, slot, rows]
        pltpu.make_async_copy(held, held, slot_recv.at[array, slot, at]).wait()

    def wait_slot(array, slot):
        for piece in pieces(array):
            wait_piece(array, slot, piece)

    def send_z(array, step, way, piece):
        @pl.when(z_wanted(step, way))
        def _():
            z_copy(array, step, way, piece).start()

    def send_t(array, spot, piece):
        for way in (1, -1):
            @pl.when(in_t(t + way))
            def _():
                t_copy(array, spot, way, piece).start()

    def send_own(array):
        for piece in pieces(array):
            send_z(array, 0, 1, piece)
            send_z(array, 0, -1, piece)

    def send_own_side(array):
        for piece in pieces(array):
            send_t(array, 2 + h, piece)

    def settle(array):
        for way in (1, -1):
            for step in range(3):
                @pl.when(z_wanted(step, way))
                def _():
                    for piece in pieces(array):
                        z_copy(array, step, way, piece).wait_send()

            for spot in range(6):
                @pl.when(in_t(t + way) & in_z(base + spot))
                def _():
                    for piece in pieces(array):
                        t_copy(array, spot, way, piece).wait_send()

    def arrive(array, step, sides=(0, 1)):
        for side in sides if step < 3 else (1,):
            for way in (1, -1):
                tile = z - way * step
                ok = in_z(tile) & (h == (side if way == 1 else 1 - side))

                @pl.when(ok)
                def _():
                    for piece in pieces(array):
                        wait_piece(array, 6 + tile - base, piece)
                        if step < 3:
                            send_z(array, step, way, piece)
                        send_t(array, tile - base, piece)

    def await_pair(arrays, dt, block):
        for spot in (2 * block, 2 * block + 1):
            @pl.when(in_t(t + dt - 1) & in_z(base + spot))
            def _():
                for array in arrays:
                    wait_slot(array, 6 * dt + spot)

    def stat_copy(spot):
        dst = 6 + h + 4 - 2 * (spot // 2)
        return pltpu.make_async_remote_copy(
            src_ref=stats.at[mine],
            dst_ref=stats.at[dst],
            send_sem=stat_send.at[6 + spot],
            recv_sem=stat_recv.at[dst],
            device_id=z_device(base + spot),
            device_id_type=MESH,
        )

    def stat_wanted(spot):
        ok = in_z(base + spot)
        return ok & (spot != 2 + h) if spot in (2, 3) else ok

    def stat_side_copy(spot, way):
        dst = 6 - 6 * way + spot
        return pltpu.make_async_remote_copy(
            src_ref=stats.at[6 + spot],
            dst_ref=stats.at[dst],
            send_sem=stat_send.at[6 + 6 * way + spot],
            recv_sem=stat_recv.at[dst],
            device_id={"ta": t + way},
            device_id_type=MESH,
        )

    def wait_stat(slot):
        pltpu.make_async_copy(stats.at[slot], stats.at[slot], stat_recv.at[slot]).wait()

    def pass_stats(spot):
        for way in (1, -1):
            @pl.when(in_t(t + way))
            def _():
                stat_side_copy(spot, way).start()

    def send_stats():
        for spot in range(6):
            @pl.when(stat_wanted(spot))
            def _():
                stat_copy(spot).start()
        pass_stats(2 + h)

    def arrive_stats():
        for spot in range(6):
            @pl.when(stat_wanted(spot))
            def _():
                wait_stat(6 + spot)
                pass_stats(spot)

    def await_stats(dt, block):
        for spot in (2 * block, 2 * block + 1):
            @pl.when(in_t(t + dt - 1) & in_z(base + spot))
            def _():
                wait_stat(6 * dt + spot)

    def pair_of(array, j, head):
        return slots[array, pl.ds(2 * j, 2), :, lanes(head)].reshape(pair, head_dim)

    def forward_pair(j):
        for head in range(heads):
            q = slots[QUERY, mine, :, lanes(head)]
            g = slots[GRAD, mine, :, lanes(head)]
            s = nt_dot(q, pair_of(KEY, j, head)) + bias[head * 9 + j]
            scores[head * 9 + j] = s
            top = peak[head]
            for at in range(0, pair, 128):
                top = jnp.maximum(top, s[:, at : at + 128])
            peak[head] = top
            probs[head * 9 + j] = nt_dot(g, pair_of(VALUE, j, head))

    def backward(head, q, g, norm, dot):
        s = nt_dot(slots[KEY, mine, :, lanes(head)], q)
        p = jnp.exp2(s * factor - norm)
        d = nt_dot(slots[VALUE, mine, :, lanes(head)], g)
        ds = (p * (d - dot)).astype(bf16)
        dv_acc[:, lanes(head)] += nn_dot(p.astype(bf16), g)
        dk_acc[:, lanes(head)] += nn_dot(ds, q)

    def backward_pair(j):
        both = jnp.concatenate([stats[2 * j, :, :tokens], stats[2 * j + 1, :, :tokens]], axis=1)
        for head in range(heads):
            norm = both[head : head + 1] - bias[head * 9 + j]
            dot = both[heads + head : heads + head + 1]
            backward(head, pair_of(QUERY, j, head), pair_of(GRAD, j, head), norm, dot)

    def backward_far(dt, step):
        slot = 6 * dt + (4 - 3 * h if step == 2 else 5 - 5 * h)

        @pl.when(in_t(t + dt - 1) & in_z(base + slot - 6 * dt))
        def _():
            wait_slot(QUERY, slot)
            wait_slot(GRAD, slot)
            wait_stat(slot)

        upper = h == (1 if step == 2 else 0)
        for head in range(heads):
            row = bias[head * 9 + 3 * dt + far]
            masks = jnp.where(upper, row[:, tokens:], row[:, :tokens])
            norm = stats[slot, head : head + 1, :tokens] - masks
            dot = stats[slot, heads + head : heads + head + 1, :tokens]
            backward(head, slots[QUERY, slot, :, lanes(head)], slots[GRAD, slot, :, lanes(head)], norm, dot)

    def early_pair(index):
        return index + h + (index >= 2 + 3 * h).astype(jnp.int32)

    def weigh(j, carry):
        for head in range(heads):
            p = jnp.exp2(scores[head * 9 + j] * factor - level[head][:, :1])
            total = totals[:, lanes(head)]
            for at in range(0, pair, 128):
                total = total + p[:, at : at + 128]
            totals[:, lanes(head)] = total
            p = p.astype(bf16)
            weights[head * 9 + j] = p
            acc[:, lanes(head)] += nn_dot(p, pair_of(VALUE, j, head))
        return carry

    def begin_softmax():
        for head in range(heads):
            top = jnp.max(peak[head], axis=1, keepdims=True) * factor
            level[head] = jnp.broadcast_to(top, (tokens, 128))
            p = jnp.exp2(text_scores[head] * factor - top)
            total = p[:, :128]
            for at in range(128, n_text, 128):
                total = total + p[:, at : at + 128]
            p = p.astype(bf16)
            text_weights[head] = p
            totals[:, lanes(head)] = total
            acc[:, lanes(head)] = nn_dot(p, text[1, :, lanes(head)])
        lax.fori_loop(0, 7, lambda index, carry: weigh(early_pair(index), carry), 0)

    def both_times(work, block):
        def body(index, carry):
            work(2 * index, block)
            return carry

        lax.fori_loop(0, 2, body, 0)

    def forward_side(dt, block):
        await_pair((KEY, VALUE), dt, block)
        forward_pair(3 * dt + block)

    def backward_side(dt, block):
        await_pair((QUERY, GRAD), dt, block)
        await_stats(dt, block)
        backward_pair(3 * dt + block)

    near, far = 2 * h, 2 - 2 * h

    for array in (KEY, VALUE):
        loads[array].wait()
        send_own(array)
        send_own_side(array)
    loads[QUERY].wait()
    send_own_side(QUERY)
    for load in loads[GRAD:]:
        load.wait()

    def zero_slot(index, carry):
        time_at, z_at = t + lax.div(index, 6) - 1, base + lax.rem(index, 6)

        @pl.when(jnp.logical_not(in_t(time_at) & in_z(z_at)))
        def _():
            for array in range(4):
                slots[array, index] = jnp.zeros((tokens, heads * head_dim), bf16)
            stats[index] = jnp.zeros((8, 256), f32)

        return carry

    lax.fori_loop(0, 18, zero_slot, 0)

    lane = lax.broadcasted_iota(jnp.int32, (1, pair), 1)
    for head in range(heads):
        reach_t, reach_h, reach_w = (window_ref[head, axis] for axis in range(3))
        for dt in range(3):
            for block in range(3):
                inside = (
                    in_t(t + dt - 1)
                    & (w + block - 1 >= 0)
                    & (w + block - 1 < n_cols)
                    & (abs(dt - 1) <= reach_t)
                    & (abs(block - 1) <= reach_w)
                )
                open_low = inside & (h <= reach_h)
                open_high = inside & (1 - h <= reach_h)
                low = jnp.where(open_low, 0.0, MASKED).astype(f32)
                high = jnp.where(open_high, 0.0, MASKED).astype(f32)
                bias[head * 9 + dt * 3 + block] = jnp.where(lane < tokens, low, high)

    for head in range(heads):
        q = slots[QUERY, mine, :, lanes(head)]
        g = slots[GRAD, mine, :, lanes(head)]
        s = nt_dot(q, text[0, :, lanes(head)])
        text_scores[head] = s
        top = s[:, :128]
        for at in range(128, n_text, 128):
            top = jnp.maximum(top, s[:, at : at + 128])
        peak[head] = top
        text_probs[head] = nt_dot(g, text[1, :, lanes(head)])
    dk_acc[...] = jnp.zeros_like(dk_acc)
    dv_acc[...] = jnp.zeros_like(dv_acc)

    arrive(KEY, 1)
    arrive(VALUE, 1)
    forward_pair(4)
    arrive(KEY, 2)
    arrive(VALUE, 2)
    send_own(QUERY)
    send_own(GRAD)
    both_times(forward_side, 1)
    forward_pair(3 + near)
    arrive(KEY, 3)
    arrive(VALUE, 3)
    both_times(forward_side, near)
    arrive(QUERY, 1, (0,))
    send_own_side(GRAD)
    forward_pair(3 + far)
    begin_softmax()
    arrive(GRAD, 1, (0,))
    both_times(forward_side, far)
    arrive(QUERY, 1, (1,))

    for head in range(heads):
        early = level[head]
        top = jnp.max(peak[head], axis=1, keepdims=True) * factor
        level[head] = jnp.broadcast_to(top, (tokens, 128))
        fade[head] = jnp.exp2(early - level[head])
        totals[:, lanes(head)] *= fade[head]
        acc[:, lanes(head)] *= fade[head]
    weigh(far, 0)
    weigh(6 + far, 0)

    row_lane = lax.broadcasted_iota(jnp.int32, (tokens, 128), 1)
    columns = jnp.zeros((tokens, 128), f32)
    inverse, dots = [], []
    for head in range(heads):
        total = jnp.sum(totals[:, lanes(head)], axis=1, keepdims=True)
        inv = 1.0 / total
        out = (acc[:, lanes(head)] * inv).astype(bf16)
        out_ref[:, lanes(head)] = out
        g = slots[GRAD, mine, :, lanes(head)].astype(f32)
        dot = jnp.sum(g * out.astype(f32), axis=1, keepdims=True)
        inverse.append(inv)
        dots.append(dot)
        columns = jnp.where(row_lane == head, level[head] + jnp.log2(total), columns)
        columns = jnp.where(row_lane == heads + head, dot, columns)
        peak[head] = jnp.broadcast_to(dot, (tokens, 128))

    own_stats = jnp.transpose(columns)[:8]
    stats[mine, :, :tokens] = own_stats
    send_stats()
    arrive(GRAD, 1, (1,))

    for head in range(heads):
        q = slots[QUERY, mine, :, lanes(head)]
        g = slots[GRAD, mine, :, lanes(head)]
        p = jnp.exp2(nt_dot(text[0, :, lanes(head)], q) * factor - own_stats[head : head + 1])
        d = nt_dot(text[1, :, lanes(head)], g)
        ds = (p * (d - own_stats[heads + head : heads + head + 1])).astype(bf16)
        dtv = nn_dot(p.astype(bf16), g).astype(bf16)
        dtk = (nn_dot(ds, q) * scale).astype(bf16)
        for part in range(n_time):
            rows = slice(part * rows_time, (part + 1) * rows_time)
            text_send[part % 2, part // 2, 0, :, lanes(head)] = dtk[rows]
            text_send[part % 2, part // 2, 1, :, lanes(head)] = dtv[rows]

    core, chip = lax.rem(t, 2), lax.div(t, 2)
    n_chips = n_time // 2
    core_copy = pltpu.make_async_remote_copy(
        src_ref=text_send.at[1 - core],
        dst_ref=text_near,
        send_sem=part_send.at[0],
        recv_sem=core_recv,
        device_id={"ta": t + 1 - 2 * core},
        device_id_type=MESH,
    )
    core_copy.start()

    def part_copy(step):
        there = lax.rem(chip + step, n_chips)
        return pltpu.make_async_remote_copy(
            src_ref=text_far.at[there],
            dst_ref=text_recv.at[chip],
            send_sem=part_send.at[step],
            recv_sem=part_recv.at[chip],
            device_id={"ta": 2 * there + core},
            device_id_type=MESH,
        )

    def sum_cores():
        core_copy.wait()
        for part in range(n_chips):
            text_far[part] = (text_send[core, part].astype(f32) + text_near[part].astype(f32)).astype(bf16)
        for step in range(1, n_chips):
            part_copy(step).start()
        text_recv[chip] = text_far[chip]

    for head in range(heads):
        ds = (text_weights[head].astype(f32) * (text_probs[head] - dots[head])).astype(bf16)
        acc[:, lanes(head)] = nn_dot(ds, text[0, :, lanes(head)])

    def pull(j, carry):
        for head in range(heads):
            dot = peak[head][:, :1]
            ds = (weights[head * 9 + j].astype(f32) * (probs[head * 9 + j] - dot)).astype(bf16)
            acc[:, lanes(head)] += nn_dot(ds, pair_of(KEY, j, head))
        return carry

    lax.fori_loop(0, 3, lambda index, carry: pull(early_pair(index), carry), 0)
    sum_cores()
    arrive(QUERY, 2)
    arrive(GRAD, 2, (0,))
    lax.fori_loop(3, 7, lambda index, carry: pull(early_pair(index), carry), 0)
    for head in range(heads):
        acc[:, lanes(head)] *= fade[head]
    pull(far, 0)
    pull(6 + far, 0)
    for head in range(heads):
        dq_ref[:, lanes(head)] = (acc[:, lanes(head)] * (inverse[head] * scale)).astype(bf16)
    arrive(GRAD, 2, (1,))
    arrive_stats()
    for step in range(1, n_chips):
        src = lax.rem(chip + step, n_chips)
        pltpu.make_async_copy(text_recv.at[src], text_recv.at[src], part_recv.at[src]).wait()
    summed = text_recv[0].astype(f32)
    for src in range(1, n_chips):
        summed = summed + text_recv[src].astype(f32)
    for part in range(n_z):
        rows = slice(part * rows_dev, (part + 1) * rows_dev)
        sum_send[part, 0:rows_dev] = summed[0, rows]
        sum_send[part, rows_dev : 2 * rows_dev] = summed[1, rows]

    def total_copy(step):
        there = lax.rem(z + step, n_z)
        to_h, to_w = lax.rem(there, n_rows), lax.div(there, n_rows)
        return pltpu.make_async_remote_copy(
            src_ref=sum_send.at[to_h * n_cols + to_w],
            dst_ref=sum_recv.at[z],
            send_sem=total_send.at[step],
            recv_sem=total_recv.at[z],
            device_id=z_device(there),
            device_id_type=MESH,
        )

    for step in range(1, n_z):
        total_copy(step).start()
    sum_recv[z] = sum_send[h * n_cols + w]


    backward_pair(4)

    backward_pair(3 + near)
    arrive(QUERY, 3)
    both_times(backward_side, 1)
    settle(KEY)
    settle(VALUE)
    arrive(GRAD, 3)
    both_times(backward_side, near)
    for dt in (0, 2):
        backward_far(dt, 2)
    backward_pair(3 + far)
    for dt in (0, 2):
        backward_far(dt, 3)

    dk_ref[...] = (dk_acc[...] * scale).astype(bf16)
    dv_ref[...] = dv_acc[...].astype(bf16)

    for step in range(1, n_z):
        src = lax.rem(z + step, n_z)
        pltpu.make_async_copy(sum_recv.at[src], sum_recv.at[src], total_recv.at[src]).wait()
    final = sum_recv[0]
    for src in range(1, n_z):
        final = final + sum_recv[src]
    dtk_ref[...] = final[0:rows_dev].astype(bf16)
    dtv_ref[...] = final[rows_dev : 2 * rows_dev].astype(bf16)

    settle(QUERY)
    settle(GRAD)
    for spot in range(6):
        @pl.when(stat_wanted(spot))
        def _():
            stat_copy(spot).wait_send()

        for way in (1, -1):
            @pl.when(in_t(t + way) & in_z(base + spot))
            def _():
                stat_side_copy(spot, way).wait_send()

    for step in range(1, n_chips):
        part_copy(step).wait_send()
    for step in range(1, n_z):
        total_copy(step).wait_send()


def finish(*refs):
    moves = [pltpu.make_async_copy(refs[at], refs[6 + at], refs[12].at[at]) for at in range(6)]
    for move in moves:
        move.start()
    for move in moves:
        move.wait()


def on_device(query, keys, values, grad_out, text_keys, text_values, window):
    bf16, f32 = jnp.bfloat16, jnp.float32
    frames, height, wide, chans = query.shape
    heads = window.shape[0]
    head_dim = chans // heads
    tokens = frames * height * wide
    n_text = text_keys.shape[0]
    n_time, n_rows, n_cols = (lax.axis_size(axis) for axis in ("ta", "ha", "wa"))
    n_z = n_rows * n_cols
    rows_time = n_text // n_time
    rows_dev = rows_time // n_z
    sizes = (n_time, n_rows, n_cols, heads, head_dim, tokens, n_text)
    pair = 2 * tokens
    tile = jax.ShapeDtypeStruct((tokens, chans), bf16)
    text = jax.ShapeDtypeStruct((rows_dev, chans), bf16)
    held = [pltpu.VMEM(leaf.shape, bf16) for leaf in (tile, tile, tile, tile, text, text)]
    anywhere = pl.BlockSpec(memory_space=pl.ANY)
    vmem = pl.BlockSpec(memory_space=pltpu.VMEM)
    dma = pltpu.SemaphoreType.DMA
    flat = [array.reshape(tokens, chans) for array in (keys, values, query, grad_out)]
    results = pl.pallas_call(
        functools.partial(kernel, sizes),
        out_shape=held,
        in_specs=[anywhere] * 7,
        out_specs=(vmem,) * 6,
        scratch_shapes=[
            pltpu.SMEM(window.shape, jnp.int32),
            pltpu.VMEM((4, 18, tokens, chans), bf16),
            pltpu.VMEM((2, n_text, chans), bf16),
            pltpu.VMEM((9 * heads, tokens, pair), f32),
            pltpu.VMEM((heads, tokens, n_text), f32),
            pltpu.VMEM((9 * heads, tokens, pair), f32),
            pltpu.VMEM((heads, tokens, n_text), f32),
            pltpu.VMEM((9 * heads, tokens, pair), bf16),
            pltpu.VMEM((heads, tokens, n_text), bf16),
            pltpu.VMEM((9 * heads, 1, pair), f32),
            pltpu.VMEM((heads, tokens, 128), f32),
            pltpu.VMEM((heads, tokens, 128), f32),
            pltpu.VMEM((heads, tokens, 128), f32),
            pltpu.VMEM((18, 8, 256), f32),
            pltpu.VMEM((tokens, chans), f32),
            pltpu.VMEM((tokens, chans), f32),
            pltpu.VMEM((tokens, chans), f32),
            pltpu.VMEM((tokens, chans), f32),
            pltpu.VMEM((2, n_time // 2, 2, rows_time, chans), bf16),
            pltpu.VMEM((n_time // 2, 2, rows_time, chans), bf16),
            pltpu.VMEM((n_time // 2, 2, rows_time, chans), bf16),
            pltpu.VMEM((n_time // 2, 2, rows_time, chans), bf16),
            pltpu.VMEM((n_z, 2 * rows_dev, chans), f32),
            pltpu.VMEM((n_z, 2 * rows_dev, chans), f32),
            dma((7,)),
            dma((4, 3, PIECES)),
            dma((4, 3, PIECES)),
            dma((4, 2, 6, PIECES)),
            dma((4, 18, PIECES)),
            dma((18,)),
            dma((18,)),
            dma,
            dma((n_time // 2,)),
            dma((n_time // 2,)),
            dma((n_z,)),
            dma((n_z,)),
        ],
        compiler_params=pltpu.CompilerParams(
            collective_id=0, has_side_effects=True, vmem_limit_bytes=56 * 1024 * 1024
        ),
    )(*flat, text_keys, text_values, window)
    out, dq, dk, dv, dtk, dtv = pl.pallas_call(
        finish,
        out_shape=(tile, tile, tile, tile, text, text),
        in_specs=[vmem] * 6,
        out_specs=(anywhere,) * 6,
        scratch_shapes=[dma((6,))],
    )(*[pltpu.with_memory_space_constraint(result, pltpu.VMEM) for result in results])
    shape = (frames, height, wide, chans)
    return tuple(array.reshape(shape) for array in (out, dq, dk, dv)) + (dtk, dtv)


def solution(mesh):
    tiled = P("ta", "ha", "wa", "head")
    placed = (tiled, tiled, tiled, tiled, P(None, "head"), P(None, "head"), P("head", None))
    text = P(("ta", "ha", "wa"), "head")
    return jax.shard_map(
        on_device,
        mesh=mesh,
        in_specs=placed,
        out_specs=(tiled, tiled, tiled, tiled, text, text),
        check_vma=False,
    )
```
